256 devices in a mesh: gx: 16 (over y, z_hi), gz: 16 (over x, z_lo, core).
Axes of the slice: x: 4, y: 4, z: 8 (z_hi: 4, z_lo: 2; z = z_hi * 2 + z_lo), core: 2. Of those that a mesh axis runs over, the one named last changes fastest.
Arguments:
- stored: bfloat16 [19, 256, 128, 256], P(None, 'gx', 'gz'), may hold values from 0 to 1, as said below
- adjoint_in: float32 [19, 256, 128, 256], P(None, 'gx', 'gz'), may hold values from -6 to 6
- marker_cell: int32 [524288], P(('gx', 'gz')), may hold values from 0 to 32767, as said below
- marker_weight: float32 [9, 524288], P(None, ('gx', 'gz')), may hold values from 0 to 1
- marker_panel: int32 [524288], P(('gx', 'gz')), may hold values from 0 to 127
- marker_count: int32 [256], P(('gx', 'gz')), may hold values from 256 to 2048, as said below
Outputs:
- adjoint_out: float32 [19, 256, 128, 256], P(None, 'gx', 'gz')
- marker_grad: float32 [3, 524288], P(None, ('gx', 'gz'))
- panel_grad: float32 [3, 128], replicated
The draws below stay inside these ranges and needn't reach their ends.
Inputs may be any that keep to these rules, and one draw needn't show every extreme that they name: marker_cell is an index within the owner tile; the base cell never lies on the grid's first or last streamwise or vertical layer. `marker_count`: some tile has all 2048 slots live in every draw. stored populations are positive.
All inputs are finite; a program needn't handle non-finite values.
Results may differ from the reference program's by a relative error of at most 0.0003.
Values sent between devices are 32-bit elements; how exact they have to be, the bound alone decides.
No kernel may reach another device: no remote copies, remote signals or barrier semaphores. Data moves between devices by JAX's collectives and lax.ppermute only.
A program may use at most 128 MiB of HBM per device.

```python
import jax
import jax.numpy as jnp
import numpy as np
from jax import lax

CX = 16
CZ = 8
NY = 256
MCAP = 2048
PANELS = 128
NX = 256
NZ = 128
NM = 524288
DEVICES = 256


def draw_stored(key, part):
    key = jax.random.fold_in(key, 11)
    first = jax.random.fold_in(key, 0)
    table = jnp.asarray(np.array([1.0 / 3.0] + [1.0 / 18.0] * 6 + [1.0 / 36.0] * 12, dtype=np.float32)).reshape(19, 1, 1, 1)
    noise = jax.random.uniform(first, (19, NX, NZ, NY), jnp.float32, 0.6, 1.4)
    scale = 1.0
    return (table * noise * scale).astype(jnp.bfloat16)


def draw_marker_cell(key, part):
    key = jax.random.fold_in(key, 12)
    first, second, third = jax.random.split(key, 3)
    rows = jnp.arange(NM, dtype=jnp.int32)
    tile = rows // MCAP
    tiles_z = NZ // CZ
    anchor_x = tile // tiles_z * CX
    anchor_z = tile % tiles_z * CZ
    local_x = jax.random.randint(first, (NM,), 0, CX, dtype=jnp.int32)
    local_z = jax.random.randint(second, (NM,), 0, CZ, dtype=jnp.int32)
    span = jax.random.randint(third, (NM,), 0, NY, dtype=jnp.int32)
    global_x = jnp.clip(anchor_x + local_x, 1, NX - 2)
    global_z = jnp.clip(anchor_z + local_z, 1, NZ - 2)
    return (((global_x - anchor_x) * CZ + (global_z - anchor_z)) * NY + span).astype(jnp.int32)


def draw_marker_count(key, part):
    key = jax.random.fold_in(key, 13)
    first, second = jax.random.split(key)
    ratio = jax.random.randint(first, (DEVICES,), 0, 8, dtype=jnp.int32)
    counts = MCAP // (1 + ratio)
    chosen = jax.random.randint(second, (), 0, DEVICES, dtype=jnp.int32)
    return jnp.where(jnp.arange(DEVICES, dtype=jnp.int32) == chosen, MCAP, counts).astype(jnp.int32)


def with_ends(values, own_key, least, high):
    spot = [jax.random.randint(jax.random.fold_in(own_key, axis), (), 0, length) for axis, length in enumerate(values.shape)]
    widest = values.shape.index(max(values.shape))
    next_to = spot[:widest] + [(spot[widest] + 1) % values.shape[widest]] + spot[widest + 1:]
    return values.at[tuple(spot)].set(least).at[tuple(next_to)].set(high)


def level_of(key, dims, shards, least, top_value):
    def one(axis_at, parts):
        steps = jax.random.uniform(jax.random.fold_in(jax.random.fold_in(key, 6), axis_at), (parts,), jnp.float32, least / len(shards), top_value / len(shards))
        return jnp.repeat(jnp.exp(steps), dims[axis_at] // parts).reshape((-1,) + (1,) * (len(dims) - axis_at - 1))

    gain = one(*shards[0])
    for cut in shards[1:]:
        gain = gain * one(*cut)
    return gain


def bell_draw(stream_key, shape, spread, reach, cuts=(), kind=jnp.bfloat16):
    values = jax.random.normal(stream_key, shape, jnp.float32) * spread
    if len(cuts) > 0:
        values = level_of(stream_key, shape, cuts, -0.22, 0.18) * values
    return jnp.clip(values, min=-reach, max=reach).astype(kind)


def setup_inputs(seed: int = 0) -> dict:
    streams_of = jax.random.split(jax.random.key(seed), 7)
    return {
        "stored": draw_stored(jax.random.fold_in(streams_of[6], 71), 0),
        "adjoint_in": bell_draw(streams_of[1], (19, NX, NZ, NY), 1.0, 6.0, ((1, 16), (2, 16)), jnp.float32),
        "marker_cell": draw_marker_cell(jax.random.fold_in(streams_of[6], 71), 0),
        "marker_weight": jnp.clip(1.0 * jax.random.uniform(streams_of[3], (9, NM), jnp.float32) ** level_of(streams_of[3], (9, NM), ((1, 256),), -0.2, 0.2), 0.0, 1.0),
        "marker_panel": with_ends(jax.random.randint(streams_of[4], (NM,), 0, PANELS), jax.random.fold_in(streams_of[4], 1), 0, PANELS - 1).astype(jnp.int32),
        "marker_count": draw_marker_count(jax.random.fold_in(streams_of[6], 71), 0),
    }


STENCIL = [(0, 0, 0), (1, 0, 0), (-1, 0, 0), (0, 1, 0), (0, -1, 0), (0, 0, 1), (0, 0, -1), (1, 1, 0), (-1, 1, 0), (1, -1, 0), (-1, -1, 0), (1, 0, 1), (-1, 0, 1), (1, 0, -1), (-1, 0, -1), (0, 1, 1), (0, -1, 1), (0, 1, -1), (0, -1, -1)]
VELOCITIES = np.array(STENCIL, dtype=np.float32)
LATTICE_WEIGHTS = np.array([1.0 / 3.0] + [1.0 / 18.0] * 6 + [1.0 / 36.0] * 12, dtype=np.float32)
RELAXATION = 1.6

def collide(pops):
    shape = (19,) + (1,) * (pops.ndim - 1)
    weights = jnp.asarray(LATTICE_WEIGHTS).astype(pops.dtype).reshape(shape)
    density = lax.optimization_barrier(jnp.sum(pops, axis=0))
    momentum = jnp.tensordot(jnp.asarray(VELOCITIES.T).astype(pops.dtype), pops, axes=1, precision=lax.Precision.HIGHEST)
    velocity = momentum / density
    along = jnp.tensordot(jnp.asarray(VELOCITIES).astype(pops.dtype), velocity, axes=1, precision=lax.Precision.HIGHEST)
    speed = lax.optimization_barrier(jnp.sum(velocity * velocity, axis=0))
    equilibrium = weights * density * (1.0 + 3.0 * along + 4.5 * along * along - 1.5 * speed)
    return pops - RELAXATION * (pops - equilibrium)

def adjoint_step(stored, pulled):
    pops = stored.astype(pulled.dtype)
    unused, backward = jax.vjp(collide, pops)
    result = backward(pulled)[0]
    shape = (19,) + (1,) * (pops.ndim - 1)
    weights = jnp.asarray(LATTICE_WEIGHTS).astype(pops.dtype).reshape(shape)
    density = lax.optimization_barrier(jnp.sum(pops, axis=0))
    sensing = 3.0 * density * jnp.tensordot(jnp.asarray(VELOCITIES.T).astype(pops.dtype), weights * pulled, axes=1, precision=lax.Precision.HIGHEST)
    return (result, sensing)

def pull(extended, width, border, extent_x, extent_z):
    pieces = []
    for step_x, step_y, step_z in STENCIL:
        low_x = width - border + step_x
        low_z = width - border + step_z
        slot = len(pieces)
        piece = extended[slot, low_x:low_x + extent_x + 2 * border, low_z:low_z + extent_z + 2 * border, :]
        if step_y != 0:
            piece = jnp.roll(piece, -step_y, axis=-1)
        pieces.append(piece)
    return jnp.stack(pieces)

def reference(stored, adjoint_in, marker_cell, marker_weight, marker_panel, marker_count):
    padded = jnp.pad(adjoint_in, ((0, 0), (1, 1), (1, 1), (0, 0)))
    pulled = pull(padded, 1, 0, NX, NZ)

    def block(index):
        start = (index * CX).astype(jnp.int32)
        part_f = lax.dynamic_slice_in_dim(stored, start, CX, 1)
        part_b = lax.dynamic_slice_in_dim(pulled, start, CX, 1)
        return adjoint_step(part_f, part_b)
    outs, sens = lax.map(block, jnp.arange(NX // CX, dtype=jnp.int32))
    adjoint_out = jnp.moveaxis(outs, 0, 1).reshape(19, NX, NZ, NY)
    sensing = jnp.moveaxis(sens, 0, 1).reshape(3, NX, NZ, NY)
    rows = jnp.arange(NM, dtype=jnp.int32)
    tile = rows // MCAP
    tiles_z = NZ // CZ
    base_x = tile // tiles_z * CX + marker_cell // (CZ * NY)
    base_z = tile % tiles_z * CZ + marker_cell // NY % CZ
    span = marker_cell % NY
    live = rows % MCAP < marker_count[tile]
    weight = jnp.where(live[None, :], marker_weight, 0.0)
    total = jnp.zeros((3, NM), jnp.float32)
    slot = 0
    for shift_x in (-1, 0, 1):
        for shift_z in (-1, 0, 1):
            total = total + weight[slot] * sensing[:, base_x + shift_x, base_z + shift_z, span]
            slot += 1
    panel = jax.ops.segment_sum(total.T, marker_panel, num_segments=PANELS).T
    return (adjoint_out, total, panel)
```

```python
import functools

import jax
import jax.numpy as jnp
from jax import lax
from jax.experimental import pallas as pl
from jax.experimental.pallas import tpu as pltpu
from jax.sharding import PartitionSpec as P

PANELS = 128
STENCIL = [
    (0, 0, 0),
    (1, 0, 0),
    (-1, 0, 0),
    (0, 1, 0),
    (0, -1, 0),
    (0, 0, 1),
    (0, 0, -1),
    (1, 1, 0),
    (-1, 1, 0),
    (1, -1, 0),
    (-1, -1, 0),
    (1, 0, 1),
    (-1, 0, 1),
    (1, 0, -1),
    (-1, 0, -1),
    (0, 1, 1),
    (0, -1, 1),
    (0, 1, -1),
    (0, -1, -1),
]
W0, W1, W2 = 1.0 / 3.0, 1.0 / 18.0, 1.0 / 36.0
WEIGHTS = [W0] + [W1] * 6 + [W2] * 12
OMEGA = 1.6

X, Z, Y = 16, 8, 256
X_UP = [q for q in range(19) if STENCIL[q][0] == 1]
X_DOWN = [q for q in range(19) if STENCIL[q][0] == -1]
Z_UP = [q for q in range(19) if STENCIL[q][2] == 1]
Z_DOWN = [q for q in range(19) if STENCIL[q][2] == -1]

ZROWS, Z_RHO, Z_MOM, Z_SPILL = 152, 80, 96, 144
XROWS, X_MOM, X_RHO, X_EDGE, X_FAR = 88, 40, 64, 72, 80

SROWS, S_LOW, S_HIGH = 192, 144, 168
CHUNK = 256


def roll_y(tile, q):
    step = STENCIL[q][1]
    if step == 0:
        return tile
    return pltpu.roll(tile, (-step) % Y, tile.ndim - 1)


def first_moments(g):
    def total(terms):
        out = None
        for q, sign in terms:
            if g[q] is None:
                continue
            if out is None:
                out = g[q] if sign > 0 else -g[q]
            else:
                out = out + g[q] if sign > 0 else out - g[q]
        return out

    parts = []
    for d in range(3):
        axis = total([(q, STENCIL[q][d]) for q in range(1, 7) if STENCIL[q][d]])
        diag = total([(q, STENCIL[q][d]) for q in range(7, 19) if STENCIL[q][d]])
        if axis is None and diag is None:
            parts.append(None)
        elif axis is None:
            parts.append(W2 * diag)
        elif diag is None:
            parts.append(W1 * axis)
        else:
            parts.append(W1 * axis + W2 * diag)
    return parts


def z_shift(tile, q, low, high):
    step = STENCIL[q][2]
    if step == 0:
        return tile
    rows = lax.broadcasted_iota(jnp.int32, tile.shape, 0)
    halo, edge = (high, Z - 1) if step > 0 else (low, 0)
    if halo is None:
        halo = jnp.zeros_like(tile)
    return jnp.where(rows == edge, halo, pltpu.roll(tile, (-step) % Z, 0))


def pulled_own(adj, q, x):
    return roll_y(z_shift(adj[q, x], q, None, None), q)


def row(ref, index):
    return ref[pl.ds(index, 1), :]


def pulled_z(adj, q, x, low, high, plane, low_on, high_on):
    step = STENCIL[q][2]
    lo = hi = None
    if step < 0:
        lo = row(low, Z_DOWN.index(q) * X + x) * low_on
    if step > 0:
        hi = row(high, Z_UP.index(q) * X + x) * high_on
    return roll_y(z_shift(adj[q, plane], q, lo, hi), q)


def ends():
    gz = lax.axis_index("gz")
    gx = lax.axis_index("gx")
    gz_n, gx_n = lax.axis_size("gz"), lax.axis_size("gx")
    flag = lambda c: jnp.where(c, 1.0, 0.0).astype(jnp.float32)
    return flag(gz > 0), flag(gz < gz_n - 1), flag(gx > 0), flag(gx < gx_n - 1)


def pack_z(stored, adj, to_low, to_high):
    def density(x):
        rho = stored[0, x].astype(jnp.float32)
        for q in range(1, 19):
            rho = rho + stored[q, x].astype(jnp.float32)
        return rho

    def column(x):
        g = [None] * 19
        for q in range(1, 19):
            at = x + STENCIL[q][0]
            if isinstance(at, int) and not 0 <= at < X:
                continue
            g[q] = pulled_own(adj, q, at)
        return first_moments(g)

    def inside(x):
        rho = density(x)
        to_low[pl.ds(Z_RHO + x, 1), :] = rho[0:1]
        to_high[pl.ds(Z_RHO + x, 1), :] = rho[Z - 1 : Z]
        for n in range(5):
            to_low[pl.ds(n * X + x, 1), :] = adj[Z_UP[n], x, 0:1, :]
            to_high[pl.ds(n * X + x, 1), :] = adj[Z_DOWN[n], x, Z - 1 : Z, :]
        for d, mom in enumerate(column(x)):
            to_low[pl.ds(Z_MOM + d * X + x, 1), :] = mom[0:1]
            to_high[pl.ds(Z_MOM + d * X + x, 1), :] = mom[Z - 1 : Z]

    inside(0)
    inside(X - 1)

    def body(x, carry):
        inside(x)
        return carry

    lax.fori_loop(1, X - 1, body, 0)
    spill = [column(-1), column(X)]
    zero = jnp.zeros((1, Y), jnp.float32)
    low_rows, high_rows = [], []
    for d in range(3):
        for side in range(2):
            mom = spill[side][d]
            low_rows.append(zero if mom is None else mom[0:1])
            high_rows.append(zero if mom is None else mom[Z - 1 : Z])
    to_low[Z_SPILL:, :] = jnp.concatenate(low_rows + [zero, zero])
    to_high[Z_SPILL:, :] = jnp.concatenate(high_rows + [zero, zero])


def shift_rows(tile, step):
    if step == 0:
        return tile
    rows = lax.broadcasted_iota(jnp.int32, tile.shape, 0)
    edge = X - 1 if step > 0 else 0
    return jnp.where(rows == edge, 0.0, pltpu.roll(tile, (-step) % X, 0))


def edge_moments(sent, pops):
    tiles, before, after = [None] * 19, [None] * 19, [None] * 19
    for n, q in enumerate(pops):
        tile = roll_y(sent[n * X : (n + 1) * X, :], q)
        step = STENCIL[q][0]
        tiles[q] = shift_rows(tile, step)
        if step > 0:
            before[q] = tile[0:1]
        if step < 0:
            after[q] = tile[X - 1 : X]
    return first_moments(tiles), first_moments(before), first_moments(after)


def plus(a, b):
    return a if b is None else a + b


def pack_x(
    stored_a, stored_b, adj_a, adj_b, sent_low, sent_high, low, high, to_left, to_right
):
    low_on, high_on, _, _ = ends()
    edge_low, edge_high = edge_moments(sent_low, Z_UP), edge_moments(sent_high, Z_DOWN)

    def side(out, adj, stored, x, plane, inner, away, skip):
        for n, q in enumerate(away):
            out[n * Z : (n + 1) * Z, :] = pulled_z(
                adj, q, x, low, high, plane, low_on, high_on
            )
        g = [None] * 19
        for q in range(1, 19):
            step = STENCIL[q][0]
            if step == 0:
                g[q] = pulled_z(adj, q, x, low, high, plane, low_on, high_on)
            elif step != skip:
                g[q] = pulled_z(adj, q, x + step, low, high, inner, low_on, high_on)
        for d, mom in enumerate(first_moments(g)):
            out[X_MOM + d * Z : X_MOM + (d + 1) * Z, :] = mom
        rho = stored[0, plane].astype(jnp.float32)
        for q in range(1, 19):
            rho = rho + stored[q, plane].astype(jnp.float32)
        out[X_RHO : X_RHO + Z, :] = rho
        beyond = 1 if x > 0 else 0
        edge, far = [], []
        for ref, own, on in ((low, edge_low, low_on), (high, edge_high, high_on)):
            for d in range(3):
                here = row(ref, Z_MOM + d * X + x) * on
                edge.append(here + own[0][d][x : x + 1])
                there = row(ref, Z_SPILL + 2 * d + beyond) * on
                far.append(plus(there, own[1 + beyond][d]))
        for ref, on in ((low, low_on), (high, high_on)):
            edge.append(row(ref, Z_RHO + x) * on)
        out[X_EDGE : X_EDGE + 8, :] = jnp.concatenate(edge)
        far = far + [jnp.zeros((1, Y), jnp.float32)] * 2
        out[X_FAR : X_FAR + 8, :] = jnp.concatenate(far)

    side(to_left, adj_a, stored_a, 0, 0, 1, X_UP, -1)
    side(to_right, adj_b, stored_b, X - 1, 1, 0, X_DOWN, 1)


def collide_transpose(f, g, emit):
    rho = f[0]
    for q in range(1, 19):
        rho = rho + f[q]
    jx = (f[1] - f[2]) + (f[7] - f[8]) + (f[9] - f[10]) + (f[11] - f[12]) + (f[13] - f[14])
    jy = (f[3] - f[4]) + (f[7] - f[9]) + (f[8] - f[10]) + (f[15] - f[16]) + (f[17] - f[18])
    jz = (f[5] - f[6]) + (f[11] - f[13]) + (f[12] - f[14]) + (f[15] - f[17]) + (f[16] - f[18])
    inv = 1.0 / rho
    ux, uy, uz = jx * inv, jy * inv, jz * inv

    sx, sy, sz = W1 * (g[1] + g[2]), W1 * (g[3] + g[4]), W1 * (g[5] + g[6])
    dx, dy, dz = W1 * (g[1] - g[2]), W1 * (g[3] - g[4]), W1 * (g[5] - g[6])

    def plane(a, b, c, d):
        p, m = g[a] + g[d], g[b] + g[c]
        r, s = g[a] - g[d], g[b] - g[c]
        return W2 * (p + m), W2 * (p - m), W2 * (r - s), W2 * (r + s)

    s_xy, c_xy, xy_x, xy_y = plane(7, 8, 9, 10)
    s_xz, c_xz, xz_x, xz_z = plane(11, 12, 13, 14)
    s_yz, c_yz, yz_y, yz_z = plane(15, 16, 17, 18)
    m_x = dx + xy_x + xz_x
    m_y = dy + xy_y + yz_y
    m_z = dz + xz_z + yz_z
    g_xx = sx + s_xy + s_xz
    g_yy = sy + s_xy + s_yz
    g_zz = sz + s_xz + s_yz
    g0 = W0 * g[0] + (sx + sy + sz) + (s_xy + s_xz + s_yz)
    vx = g_xx * ux + c_xy * uy + c_xz * uz
    vy = c_xy * ux + g_yy * uy + c_yz * uz
    vz = c_xz * ux + c_yz * uy + g_zz * uz
    uv = ux * vx + uy * vy + uz * vz
    uu = ux * ux + uy * uy + uz * uz
    base = OMEGA * (g0 - 4.5 * uv + 1.5 * uu * g0)
    bx = OMEGA * (3.0 * m_x + 9.0 * vx - 3.0 * ux * g0)
    by = OMEGA * (3.0 * m_y + 9.0 * vy - 3.0 * uy * g0)
    bz = OMEGA * (3.0 * m_z + 9.0 * vz - 3.0 * uz * g0)
    xp, xm = base + bx, base - bx
    yp, ym = base + by, base - by
    along = {
        (0, 0, 0): base,
        (1, 0, 0): xp,
        (-1, 0, 0): xm,
        (0, 1, 0): yp,
        (0, -1, 0): ym,
        (0, 0, 1): base + bz,
        (0, 0, -1): base - bz,
        (1, 1, 0): xp + by,
        (-1, 1, 0): xm + by,
        (1, -1, 0): xp - by,
        (-1, -1, 0): xm - by,
        (1, 0, 1): xp + bz,
        (-1, 0, 1): xm + bz,
        (1, 0, -1): xp - bz,
        (-1, 0, -1): xm - bz,
        (0, 1, 1): yp + bz,
        (0, -1, 1): ym + bz,
        (0, 1, -1): yp - bz,
        (0, -1, -1): ym - bz,
    }
    for q in range(19):
        emit(q, along[STENCIL[q]] + (1.0 - OMEGA) * g[q])
    scale = 3.0 * rho
    return scale * m_x, scale * m_y, scale * m_z


def interior(stored, adj, low, high, out, sens):
    low_on, high_on, _, _ = ends()

    def body(x, carry):
        f = [stored[q, x].astype(jnp.float32) for q in range(19)]
        g = []
        for q in range(19):
            at = x + STENCIL[q][0]
            g.append(pulled_z(adj, q, at, low, high, at, low_on, high_on))

        def emit(q, value):
            out[q, x] = value

        for d, tile in enumerate(collide_transpose(f, g, emit)):
            sens[d, pl.ds(pl.multiple_of(x * Z, Z), Z), :] = tile
        return carry

    lax.fori_loop(1, X - 1, body, 0)
    zero = jnp.zeros((Z, Y), jnp.float32)
    for q in range(19):
        out[q, 0] = zero
        out[q, X - 1] = zero
    for d in range(3):
        sens[d, 0:Z, :] = zero
        sens[d, (X - 1) * Z :, :] = zero


def finish(
    count,
    stored_a,
    stored_b,
    adj_a,
    adj_b,
    sent_low,
    sent_high,
    low,
    high,
    sent_left,
    sent_right,
    left,
    right,
    sens_in,
    cell,
    panel,
    weight,
    out_in,
    out,
    grad,
    partial,
    planes,
    sens,
    split,
    sems,
):
    del out_in
    low_on, high_on, left_on, right_on = ends()

    copies = []
    for x, adj, stored, plane, inner, taken, ref, on in (
        (0, adj_a, stored_a, 0, 1, X_DOWN, left, left_on),
        (X - 1, adj_b, stored_b, 1, 0, X_UP, right, right_on),
    ):
        f = [stored[q, plane].astype(jnp.float32) for q in range(19)]
        g = []
        for q in range(19):
            step = STENCIL[q][0]
            if q in taken:
                n = taken.index(q)
                g.append(ref[n * Z : (n + 1) * Z, :] * on)
            else:
                at = plane if step == 0 else inner
                g.append(pulled_z(adj, q, x + step, low, high, at, low_on, high_on))

        def emit(q, value, plane=plane):
            planes[plane, q] = value

        for d, tile in enumerate(collide_transpose(f, g, emit)):
            sens[pl.ds(d * SROWS + x * Z, Z), :] = tile
        copy = pltpu.make_async_copy(planes.at[plane], out.at[:, x], sems.at[plane])
        copy.start()
        copies.append(copy)

    for d in range(3):
        sens[d * SROWS + Z : d * SROWS + (X - 1) * Z, :] = sens_in[d, Z : (X - 1) * Z, :]

    for slot, sent, ref, pops in (
        (X, sent_left, left, X_UP),
        (X + 1, sent_right, right, X_DOWN),
    ):
        g = [None] * 19
        for n, q in enumerate(pops):
            g[q] = sent[n * Z : (n + 1) * Z, :]
        scale = 3.0 * ref[X_RHO : X_RHO + Z, :]
        for d, mom in enumerate(first_moments(g)):
            tile = scale * (ref[X_MOM + d * Z : X_MOM + (d + 1) * Z, :] + mom)
            sens[d * SROWS + slot * Z : d * SROWS + (slot + 1) * Z, :] = tile

    for k, (own, pops, ref, on, start) in enumerate(
        (
            (sent_low, Z_UP, low, low_on, S_LOW),
            (sent_high, Z_DOWN, high, high_on, S_HIGH),
        )
    ):
        moments, _, _ = edge_moments(own, pops)
        rows = lax.broadcasted_iota(jnp.int32, (X, Y), 0)
        scale = 3.0 * ref[Z_RHO : Z_RHO + X, :] * on
        for d in range(3):
            far_left = left[X_FAR + 3 * k + d : X_FAR + 3 * k + d + 1, :] * left_on
            far_right = right[X_FAR + 3 * k + d : X_FAR + 3 * k + d + 1, :] * right_on
            mom = moments[d] + ref[Z_MOM + d * X : Z_MOM + (d + 1) * X, :]
            mom = mom + jnp.where(rows == 0, far_left, 0.0)
            mom = mom + jnp.where(rows == X - 1, far_right, 0.0)
            sens[d * SROWS + start : d * SROWS + start + X, :] = scale * mom
            ends_rows = []
            for mine, theirs in ((sent_left, left), (sent_right, right)):
                rho = theirs[X_EDGE + 6 + k : X_EDGE + 7 + k, :]
                at = X_EDGE + 3 * k + d
                far = X_FAR + 3 * k + d
                ends_rows.append(3.0 * rho * (theirs[at : at + 1, :] + mine[far : far + 1, :]))
            ends_rows.append(jnp.zeros((6, Y), jnp.float32))
            sens[d * SROWS + start + X : d * SROWS + start + X + 8, :] = jnp.concatenate(
                ends_rows
            )

    value = sens[...]
    head = value.astype(jnp.bfloat16)
    split[:, 0:Y] = head
    split[:, Y : 2 * Y] = (value - head.astype(jnp.float32)).astype(jnp.bfloat16)

    sub = lax.broadcasted_iota(jnp.int32, (8, CHUNK), 0)
    edge_x = [sub, sub + 8, jnp.where(sub == 0, -1, jnp.where(sub == 1, X, -9))]
    lanes = lax.broadcasted_iota(jnp.int32, (1, CHUNK), 1)

    def chunk(c, acc):
        start = pl.multiple_of(c * CHUNK, CHUNK)
        where = pl.ds(start, CHUNK)
        cells = cell[:, where]
        base_x = cells >> 11
        base_z = (cells >> 8) & 7
        live = (lanes + start) < count[0]
        w = [jnp.where(live, weight[s : s + 1, where], 0.0) for s in range(9)]

        y_of = jnp.broadcast_to(cells & 255, (Y, CHUNK))
        hot = jnp.where(lax.broadcasted_iota(jnp.int32, (Y, CHUNK), 0) == y_of, 1.0, 0.0)
        hot = hot.astype(jnp.bfloat16)
        hot = jnp.concatenate([hot, hot])

        bx = jnp.broadcast_to(base_x, (8, CHUNK))
        bz = jnp.broadcast_to(base_z, (8, CHUNK))
        dz = sub - bz
        inner, lower, upper = [], [], []
        for a in range(3):
            wa = [jnp.broadcast_to(w[3 * a + b], (8, CHUNK)) for b in range(3)]
            inner.append(
                jnp.where(
                    dz == -1, wa[0], jnp.where(dz == 0, wa[1], jnp.where(dz == 1, wa[2], 0.0))
                )
            )
            lower.append(jnp.where(bz == 0, wa[0], 0.0))
            upper.append(jnp.where(bz == Z - 1, wa[2], 0.0))

        def pick(at, three):
            dx = at - bx
            return jnp.where(
                dx == -1, three[0], jnp.where(dx == 0, three[1], jnp.where(dx == 1, three[2], 0.0))
            )

        factors = [pick(x, inner) for x in list(range(X)) + [-1, X]]
        factors += [pick(at, lower) for at in edge_x]
        factors += [pick(at, upper) for at in edge_x]
        totals = []
        for d in range(3):
            picked = jnp.dot(
                split[d * SROWS : (d + 1) * SROWS, :], hot, preferred_element_type=jnp.float32
            )
            summed = factors[0] * picked[0:8]
            for t in range(1, SROWS // 8):
                summed = summed + factors[t] * picked[8 * t : 8 * t + 8]
            totals.append(jnp.sum(summed, axis=0, keepdims=True))
            grad[d : d + 1, where] = totals[d]
        rows = jnp.concatenate(totals + [jnp.zeros((5, CHUNK), jnp.float32)])
        top = rows.astype(jnp.bfloat16)
        rest = (rows - top.astype(jnp.float32)).astype(jnp.bfloat16)
        panels = jnp.broadcast_to(panel[:, where], (PANELS, CHUNK))
        which = lax.broadcasted_iota(jnp.int32, (PANELS, CHUNK), 0) == panels
        which = jnp.where(which, 1.0, 0.0).astype(jnp.bfloat16)
        both = jnp.concatenate([top, rest])
        return acc + lax.dot_general(
            both, which, (((1,), (1,)), ((), ())), preferred_element_type=jnp.float32
        )

    acc = lax.fori_loop(
        0, cell.shape[1] // CHUNK, chunk, jnp.zeros((16, PANELS), jnp.float32)
    )
    result = acc[0:3] + acc[8:11]
    for n in range(partial.shape[0]):
        partial[n] = result
    for copy in copies:
        copy.wait()


def ring(axis, step):
    count = lax.axis_size(axis)
    return [(i, (i + step) % count) for i in range(count)]


PARAMS = pltpu.CompilerParams(vmem_limit_bytes=48 * 1024 * 1024)


def cost(flops, moved):
    return pl.CostEstimate(flops=flops, bytes_accessed=moved, transcendentals=0)


def shape(*dims):
    return jax.ShapeDtypeStruct(dims, jnp.float32)


def pair(low):
    index = 0 if low else X // 2 - 1
    return pl.BlockSpec((19, 2, Z, Y), lambda i: (0, index, 0, 0))


def local(stored, adjoint_in, marker_cell, marker_weight, marker_panel, marker_count):
    slots = marker_cell.shape[0]
    whole = pl.BlockSpec(memory_space=pltpu.VMEM)
    to_low, to_high = pl.pallas_call(
        pack_z,
        out_shape=(shape(ZROWS, Y), shape(ZROWS, Y)),
        compiler_params=PARAMS,
        cost_estimate=cost(5_000_000, 4_000_000),
    )(stored, adjoint_in)
    low = lax.ppermute(to_high, "gz", ring("gz", 1))
    high = lax.ppermute(to_low, "gz", ring("gz", -1))
    to_left, to_right = pl.pallas_call(
        pack_x,
        grid=(1,),
        out_shape=(shape(XROWS, Y), shape(XROWS, Y)),
        in_specs=[pair(True), pair(False), pair(True), pair(False)] + [whole] * 4,
        compiler_params=PARAMS,
        cost_estimate=cost(1_000_000, 2_000_000),
    )(stored, stored, adjoint_in, adjoint_in, to_low, to_high, low, high)
    left = lax.ppermute(to_right, "gx", ring("gx", 1))
    right = lax.ppermute(to_left, "gx", ring("gx", -1))
    out, sens = pl.pallas_call(
        interior,
        out_shape=(shape(19, X, Z, Y), shape(3, X * Z, Y)),
        compiler_params=PARAMS,
        cost_estimate=cost(10_000_000, 7_000_000),
    )(stored, adjoint_in, low, high)
    any_space = pl.BlockSpec(memory_space=pl.ANY)
    out, grad, partial = pl.pallas_call(
        finish,
        grid=(1,),
        out_shape=(
            shape(19, X, Z, Y),
            shape(3, slots),
            shape(lax.axis_size("gz"), 3, PANELS),
        ),
        in_specs=[pl.BlockSpec(memory_space=pltpu.SMEM)]
        + [pair(True), pair(False), pair(True), pair(False)]
        + [whole] * 12
        + [any_space],
        out_specs=(any_space, whole, whole),
        scratch_shapes=[
            pltpu.VMEM((2, 19, Z, Y), jnp.float32),
            pltpu.VMEM((3 * SROWS, Y), jnp.float32),
            pltpu.VMEM((3 * SROWS, 2 * Y), jnp.bfloat16),
            pltpu.SemaphoreType.DMA((2,)),
        ],
        input_output_aliases={17: 0},
        compiler_params=PARAMS,
        cost_estimate=cost(1_000_000_000, 4_000_000),
    )(
        marker_count,
        stored,
        stored,
        adjoint_in,
        adjoint_in,
        to_low,
        to_high,
        low,
        high,
        to_left,
        to_right,
        left,
        right,
        sens,
        marker_cell.reshape(1, slots),
        marker_panel.reshape(1, slots),
        marker_weight,
        out,
    )
    total = jnp.sum(lax.all_to_all(partial, "gz", 0, 0), axis=0)
    copies = jnp.broadcast_to(total[None], (lax.axis_size("gx"),) + total.shape)
    total = jnp.sum(lax.all_to_all(copies, "gx", 0, 0), axis=0)
    return (out, grad, total)


def solution(mesh):
    return jax.shard_map(
        local,
        mesh=mesh,
        in_specs=(
            P(None, "gx", "gz", None),
            P(None, "gx", "gz", None),
            P(("gx", "gz")),
            P(None, ("gx", "gz")),
            P(("gx", "gz")),
            P(("gx", "gz")),
        ),
        out_specs=(P(None, "gx", "gz", None), P(None, ("gx", "gz")), P()),
        check_vma=False,
    )
```

```python
import functools

import jax
import jax.numpy as jnp
from jax import lax
from jax.experimental import pallas as pl
from jax.experimental.pallas import tpu as pltpu
from jax.sharding import PartitionSpec as P

PANELS = 128
STENCIL = [
    (0, 0, 0),
    (1, 0, 0),
    (-1, 0, 0),
    (0, 1, 0),
    (0, -1, 0),
    (0, 0, 1),
    (0, 0, -1),
    (1, 1, 0),
    (-1, 1, 0),
    (1, -1, 0),
    (-1, -1, 0),
    (1, 0, 1),
    (-1, 0, 1),
    (1, 0, -1),
    (-1, 0, -1),
    (0, 1, 1),
    (0, -1, 1),
    (0, 1, -1),
    (0, -1, -1),
]
W0, W1, W2 = 1.0 / 3.0, 1.0 / 18.0, 1.0 / 36.0
WEIGHTS = [W0] + [W1] * 6 + [W2] * 12
OMEGA = 1.6

X, Z, Y = 16, 8, 256
X_UP = [q for q in range(19) if STENCIL[q][0] == 1]
X_DOWN = [q for q in range(19) if STENCIL[q][0] == -1]
Z_UP = [q for q in range(19) if STENCIL[q][2] == 1]
Z_DOWN = [q for q in range(19) if STENCIL[q][2] == -1]

ZROWS, Z_RHO, Z_MOM, Z_SPILL = 152, 80, 96, 144
XROWS, X_MOM, X_RHO, X_EDGE, X_FAR = 88, 40, 64, 72, 80

CHUNK = 256
UNROLL_C = 8
GROUPS = 4
STEP = X // GROUPS


def roll_y(tile, q):
    step = STENCIL[q][1]
    if step == 0:
        return tile
    return pltpu.roll(tile, (-step) % Y, tile.ndim - 1)


def first_moments(g):
    def total(terms):
        out = None
        for q, sign in terms:
            if g[q] is None:
                continue
            if out is None:
                out = g[q] if sign > 0 else -g[q]
            else:
                out = out + g[q] if sign > 0 else out - g[q]
        return out

    parts = []
    for d in range(3):
        axis = total([(q, STENCIL[q][d]) for q in range(1, 7) if STENCIL[q][d]])
        diag = total([(q, STENCIL[q][d]) for q in range(7, 19) if STENCIL[q][d]])
        if axis is None and diag is None:
            parts.append(None)
        elif axis is None:
            parts.append(W2 * diag)
        elif diag is None:
            parts.append(W1 * axis)
        else:
            parts.append(W1 * axis + W2 * diag)
    return parts


def z_shift(tile, q, low, high):
    step = STENCIL[q][2]
    if step == 0:
        return tile
    rows = lax.broadcasted_iota(jnp.int32, tile.shape, 0)
    halo, edge = (high, Z - 1) if step > 0 else (low, 0)
    if halo is None:
        halo = jnp.zeros_like(tile)
    return jnp.where(rows == edge, halo, pltpu.roll(tile, (-step) % Z, 0))


def pulled_own(adj, q, x):
    return roll_y(z_shift(adj[q, x], q, None, None), q)


def row(ref, index):
    return ref[pl.ds(index, 1), :]


def pulled_z(adj, q, x, low, high, plane, low_on, high_on):
    step = STENCIL[q][2]
    lo = hi = None
    if step < 0:
        lo = row(low, Z_DOWN.index(q) * X + x) * low_on
    if step > 0:
        hi = row(high, Z_UP.index(q) * X + x) * high_on
    return roll_y(z_shift(adj[q, plane], q, lo, hi), q)


def ends():
    gz = lax.axis_index("gz")
    gx = lax.axis_index("gx")
    gz_n, gx_n = lax.axis_size("gz"), lax.axis_size("gx")
    flag = lambda c: jnp.where(c, 1.0, 0.0).astype(jnp.float32)
    return flag(gz > 0), flag(gz < gz_n - 1), flag(gx > 0), flag(gx < gx_n - 1)


def pack_z(stored_in, adj_in, to_low, to_high, mom_out, rho_out, stored, adj, sems):
    copies = []
    for n in range(GROUPS):
        part = pl.ds(n * STEP, STEP)
        for k, (src, dst) in enumerate(((adj_in, adj), (stored_in, stored))):
            copy = pltpu.make_async_copy(src.at[:, part], dst.at[:, part], sems.at[k, n])
            copy.start()
            copies.append(copy)

    def column(x):
        g = [None] * 19
        for q in range(1, 19):
            at = x + STENCIL[q][0]
            if isinstance(at, int) and not 0 <= at < X:
                continue
            g[q] = pulled_own(adj, q, at)
        return first_moments(g)

    def density(x):
        rho = stored[0, x].astype(jnp.float32)
        for q in range(1, 19):
            rho = rho + stored[q, x].astype(jnp.float32)
        rho_out[pl.ds(x * Z, Z), :] = rho
        to_low[pl.ds(Z_RHO + x, 1), :] = rho[0:1]
        to_high[pl.ds(Z_RHO + x, 1), :] = rho[Z - 1 : Z]
        for n in range(5):
            to_low[pl.ds(n * X + x, 1), :] = adj[Z_UP[n], x, 0:1, :]
            to_high[pl.ds(n * X + x, 1), :] = adj[Z_DOWN[n], x, Z - 1 : Z, :]

    def moments(x):
        for d, mom in enumerate(column(x)):
            mom_out[d, pl.ds(x * Z, Z), :] = mom
            to_low[pl.ds(Z_MOM + d * X + x, 1), :] = mom[0:1]
            to_high[pl.ds(Z_MOM + d * X + x, 1), :] = mom[Z - 1 : Z]

    for n in range(GROUPS):
        copies[2 * n].wait()
        copies[2 * n + 1].wait()
        first, last = n * STEP, (n + 1) * STEP
        for x in range(first, last):
            density(x)
        for x in range(max(first - 1, 0), last if n == GROUPS - 1 else last - 1):
            moments(x)
    spill = [column(-1), column(X)]
    zero = jnp.zeros((1, Y), jnp.float32)
    low_rows, high_rows = [], []
    for d in range(3):
        for side in range(2):
            mom = spill[side][d]
            low_rows.append(zero if mom is None else mom[0:1])
            high_rows.append(zero if mom is None else mom[Z - 1 : Z])
    to_low[Z_SPILL:, :] = jnp.concatenate(low_rows + [zero, zero])
    to_high[Z_SPILL:, :] = jnp.concatenate(high_rows + [zero, zero])


def shift_rows(tile, step):
    if step == 0:
        return tile
    rows = lax.broadcasted_iota(jnp.int32, tile.shape, 0)
    edge = X - 1 if step > 0 else 0
    return jnp.where(rows == edge, 0.0, pltpu.roll(tile, (-step) % X, 0))


def edge_moments(sent, pops):
    tiles, before, after = [None] * 19, [None] * 19, [None] * 19
    for n, q in enumerate(pops):
        tile = roll_y(sent[n * X : (n + 1) * X, :], q)
        step = STENCIL[q][0]
        tiles[q] = shift_rows(tile, step)
        if step > 0:
            before[q] = tile[0:1]
        if step < 0:
            after[q] = tile[X - 1 : X]
    return first_moments(tiles), first_moments(before), first_moments(after)


def plus(a, b):
    return a if b is None else a + b


def pack_x(
    stored_a,
    stored_b,
    adj_a,
    adj_b,
    sent_low,
    sent_high,
    low,
    high,
    after,
    to_left,
    to_right,
):
    del after
    low_on, high_on, _, _ = ends()
    edge_low, edge_high = edge_moments(sent_low, Z_UP), edge_moments(sent_high, Z_DOWN)

    def side(out, adj, stored, x, plane, inner, away, skip):
        for n, q in enumerate(away):
            out[n * Z : (n + 1) * Z, :] = pulled_z(
                adj, q, x, low, high, plane, low_on, high_on
            )
        g = [None] * 19
        for q in range(1, 19):
            step = STENCIL[q][0]
            if step == 0:
                g[q] = pulled_z(adj, q, x, low, high, plane, low_on, high_on)
            elif step != skip:
                g[q] = pulled_z(adj, q, x + step, low, high, inner, low_on, high_on)
        for d, mom in enumerate(first_moments(g)):
            out[X_MOM + d * Z : X_MOM + (d + 1) * Z, :] = mom
        rho = stored[0, plane].astype(jnp.float32)
        for q in range(1, 19):
            rho = rho + stored[q, plane].astype(jnp.float32)
        out[X_RHO : X_RHO + Z, :] = rho
        beyond = 1 if x > 0 else 0
        edge, far = [], []
        for ref, own, on in ((low, edge_low, low_on), (high, edge_high, high_on)):
            for d in range(3):
                here = row(ref, Z_MOM + d * X + x) * on
                edge.append(here + own[0][d][x : x + 1])
                there = row(ref, Z_SPILL + 2 * d + beyond) * on
                far.append(plus(there, own[1 + beyond][d]))
        for ref, on in ((low, low_on), (high, high_on)):
            edge.append(row(ref, Z_RHO + x) * on)
        out[X_EDGE : X_EDGE + 8, :] = jnp.concatenate(edge)
        far = far + [jnp.zeros((1, Y), jnp.float32)] * 2
        out[X_FAR : X_FAR + 8, :] = jnp.concatenate(far)

    side(to_left, adj_a, stored_a, 0, 0, 1, X_UP, -1)
    side(to_right, adj_b, stored_b, X - 1, 1, 0, X_DOWN, 1)


def collide_transpose(f, g, emit):
    rho = f[0]
    for q in range(1, 19):
        rho = rho + f[q]
    jx = (f[1] - f[2]) + (f[7] - f[8]) + (f[9] - f[10]) + (f[11] - f[12]) + (f[13] - f[14])
    jy = (f[3] - f[4]) + (f[7] - f[9]) + (f[8] - f[10]) + (f[15] - f[16]) + (f[17] - f[18])
    jz = (f[5] - f[6]) + (f[11] - f[13]) + (f[12] - f[14]) + (f[15] - f[17]) + (f[16] - f[18])
    inv = 1.0 / rho
    ux, uy, uz = jx * inv, jy * inv, jz * inv

    sx, sy, sz = W1 * (g[1] + g[2]), W1 * (g[3] + g[4]), W1 * (g[5] + g[6])
    dx, dy, dz = W1 * (g[1] - g[2]), W1 * (g[3] - g[4]), W1 * (g[5] - g[6])

    def plane(a, b, c, d):
        p, m = g[a] + g[d], g[b] + g[c]
        r, s = g[a] - g[d], g[b] - g[c]
        return W2 * (p + m), W2 * (p - m), W2 * (r - s), W2 * (r + s)

    s_xy, c_xy, xy_x, xy_y = plane(7, 8, 9, 10)
    s_xz, c_xz, xz_x, xz_z = plane(11, 12, 13, 14)
    s_yz, c_yz, yz_y, yz_z = plane(15, 16, 17, 18)
    m_x = dx + xy_x + xz_x
    m_y = dy + xy_y + yz_y
    m_z = dz + xz_z + yz_z
    g_xx = sx + s_xy + s_xz
    g_yy = sy + s_xy + s_yz
    g_zz = sz + s_xz + s_yz
    g0 = W0 * g[0] + (sx + sy + sz) + (s_xy + s_xz + s_yz)
    vx = g_xx * ux + c_xy * uy + c_xz * uz
    vy = c_xy * ux + g_yy * uy + c_yz * uz
    vz = c_xz * ux + c_yz * uy + g_zz * uz
    uv = ux * vx + uy * vy + uz * vz
    uu = ux * ux + uy * uy + uz * uz
    base = OMEGA * (g0 - 4.5 * uv + 1.5 * uu * g0)
    bx = OMEGA * (3.0 * m_x + 9.0 * vx - 3.0 * ux * g0)
    by = OMEGA * (3.0 * m_y + 9.0 * vy - 3.0 * uy * g0)
    bz = OMEGA * (3.0 * m_z + 9.0 * vz - 3.0 * uz * g0)
    xp, xm = base + bx, base - bx
    yp, ym = base + by, base - by
    along = {
        (0, 0, 0): base,
        (1, 0, 0): xp,
        (-1, 0, 0): xm,
        (0, 1, 0): yp,
        (0, -1, 0): ym,
        (0, 0, 1): base + bz,
        (0, 0, -1): base - bz,
        (1, 1, 0): xp + by,
        (-1, 1, 0): xm + by,
        (1, -1, 0): xp - by,
        (-1, -1, 0): xm - by,
        (1, 0, 1): xp + bz,
        (-1, 0, 1): xm + bz,
        (1, 0, -1): xp - bz,
        (-1, 0, -1): xm - bz,
        (0, 1, 1): yp + bz,
        (0, -1, 1): ym + bz,
        (0, 1, -1): yp - bz,
        (0, -1, -1): ym - bz,
    }
    for q in range(19):
        emit(q, along[STENCIL[q]] + (1.0 - OMEGA) * g[q])


def interior(stored, adj, low, high, out):
    low_on, high_on, _, _ = ends()

    def body(x, carry):
        f = [stored[q, x].astype(jnp.float32) for q in range(19)]
        g = []
        for q in range(19):
            at = x + STENCIL[q][0]
            g.append(pulled_z(adj, q, at, low, high, at, low_on, high_on))

        def emit(q, value):
            out[q, x] = value

        collide_transpose(f, g, emit)
        return carry

    lax.fori_loop(1, X - 1, body, 0)
    zero = jnp.zeros((Z, Y), jnp.float32)
    for q in range(19):
        out[q, 0] = zero
        out[q, X - 1] = zero


def borders(stored_a, stored_b, adj_a, adj_b, low, high, left, right, out_in, out, planes, sems):
    del out_in
    low_on, high_on, left_on, right_on = ends()
    copies = []
    for x, adj, stored, plane, inner, taken, ref, on in (
        (0, adj_a, stored_a, 0, 1, X_DOWN, left, left_on),
        (X - 1, adj_b, stored_b, 1, 0, X_UP, right, right_on),
    ):
        f = [stored[q, plane].astype(jnp.float32) for q in range(19)]
        g = []
        for q in range(19):
            step = STENCIL[q][0]
            if q in taken:
                n = taken.index(q)
                g.append(ref[n * Z : (n + 1) * Z, :] * on)
            else:
                at = plane if step == 0 else inner
                g.append(pulled_z(adj, q, x + step, low, high, at, low_on, high_on))

        def emit(q, value, plane=plane):
            planes[plane, q] = value

        collide_transpose(f, g, emit)
        copy = pltpu.make_async_copy(planes.at[plane], out.at[:, x], sems.at[plane])
        copy.start()
        copies.append(copy)
    for copy in copies:
        copy.wait()


def put(split, at, tile):
    head = tile.astype(jnp.bfloat16)
    split[pl.ds(at, tile.shape[0]), :] = head
    rest = (tile - head.astype(jnp.float32)).astype(jnp.bfloat16)
    split[pl.ds(split.shape[0] // 2 + at, tile.shape[0]), :] = rest


def bases(cell, where):
    cells = cell[:, where]
    bx = jnp.broadcast_to(cells >> 11, (8, CHUNK))
    bz = jnp.broadcast_to((cells >> 8) & 7, (8, CHUNK))
    return bx, bz


def pick(dx, three):
    return jnp.where(
        dx == -1, three[0], jnp.where(dx == 0, three[1], jnp.where(dx == 1, three[2], 0.0))
    )


def gathered(split, rows, hot, factors):
    picked = jnp.dot(split[...], hot, preferred_element_type=jnp.float32)
    half = split.shape[0] // 2
    out = []
    for d in range(3):
        summed = None
        for t, factor in enumerate(factors):
            at = d * rows + 8 * t
            term = factor * (picked[at : at + 8] + picked[half + at : half + at + 8])
            summed = term if summed is None else summed + term
        out.append(summed)
    return out


def sublanes():
    return lax.broadcasted_iota(jnp.int32, (8, CHUNK), 0)


def chunk_of(c):
    return pl.ds(pl.multiple_of(c * CHUNK, CHUNK), CHUNK)


def weights_of(weight, where):
    return [jnp.broadcast_to(weight[s : s + 1, where], (8, CHUNK)) for s in range(9)]


def stage_a(count, mom, rho, cell, weight, live_weight, hot, acc, split):
    rows = X * Z
    for x in range(0, X, 2):
        scale = 3.0 * rho[x * Z : (x + 2) * Z, :]
        for d in range(3):
            put(split, d * rows + x * Z, scale * mom[d, x * Z : (x + 2) * Z, :])
    lanes = lax.broadcasted_iota(jnp.int32, (9, CHUNK), 1)

    def chunk(c, carry):
        where = chunk_of(c)
        live = (lanes + c * CHUNK) < count[0]
        live_weight[:, where] = jnp.where(live, weight[:, where], 0.0)
        w = weights_of(live_weight, where)
        y_of = jnp.broadcast_to(cell[:, where] & (Y - 1), (Y, CHUNK))
        one = jnp.where(lax.broadcasted_iota(jnp.int32, (Y, CHUNK), 0) == y_of, 1.0, 0.0)
        one = one.astype(jnp.bfloat16)
        hot[:, where] = one
        bx, bz = bases(cell, where)
        dz = sublanes() - bz
        three = [pick(dz, w[3 * a : 3 * a + 3]) for a in range(3)]
        factors = [pick(x - bx, three) for x in range(X)]
        for d, tile in enumerate(gathered(split, rows, one, factors)):
            acc[d, :, where] = tile
        return carry

    lax.fori_loop(0, cell.shape[1] // CHUNK, chunk, 0)


def stage_b(
    sent_low, sent_high, low, high, cell, panel, weight, hot, acc_in, acc, which, split
):
    low_on, high_on, _, _ = ends()
    rows = 4 * X
    for k, (sent, up, back, ref, on) in enumerate(
        (
            (sent_low, Z_UP, Z_DOWN, low, low_on),
            (sent_high, Z_DOWN, Z_UP, high, high_on),
        )
    ):
        beyond, _, _ = edge_moments(sent, up)
        added, _, _ = edge_moments(ref, back)
        here = 3.0 * sent[Z_RHO : Z_RHO + X, :] * on
        there = 3.0 * ref[Z_RHO : Z_RHO + X, :]
        for d in range(3):
            put(split, d * rows + k * X, here * added[d])
            mom = beyond[d] + ref[Z_MOM + d * X : Z_MOM + (d + 1) * X, :]
            put(split, d * rows + (2 + k) * X, there * mom)

    def chunk(c, carry):
        where = chunk_of(c)
        w = weights_of(weight, where)
        bx, bz = bases(cell, where)
        sub = sublanes()
        dx = [sub - bx, sub + 8 - bx]
        first, last, under, over = [], [], [], []
        for a in range(3):
            wa = w[3 * a : 3 * a + 3]
            first.append(jnp.where(bz == 0, wa[1], jnp.where(bz == 1, wa[0], 0.0)))
            last.append(jnp.where(bz == Z - 1, wa[1], jnp.where(bz == Z - 2, wa[2], 0.0)))
            under.append(jnp.where(bz == 0, wa[0], 0.0))
            over.append(jnp.where(bz == Z - 1, wa[2], 0.0))
        factors = [pick(at, three) for three in (first, last, under, over) for at in dx]
        for d, tile in enumerate(gathered(split, rows, hot[:, where], factors)):
            acc[d, :, where] = acc_in[d, :, where] + tile
        panels = jnp.broadcast_to(panel[:, where], (PANELS, CHUNK))
        match = lax.broadcasted_iota(jnp.int32, (PANELS, CHUNK), 0) == panels
        which[:, where] = jnp.where(match, 1.0, 0.0).astype(jnp.bfloat16)
        return carry

    lax.fori_loop(0, cell.shape[1] // CHUNK, chunk, 0)


def stage_c(
    rho,
    sent_left,
    sent_right,
    low,
    high,
    left,
    right,
    cell,
    weight,
    hot,
    which,
    acc_in,
    grad,
    partial,
    split,
    totals,
):
    low_on, high_on, left_on, right_on = ends()
    rows = 48
    zero = jnp.zeros((8, Y), jnp.float32)
    beyond, added = [], []
    for sent, ref, on, pops, back, x in (
        (sent_left, left, left_on, X_UP, X_DOWN, 0),
        (sent_right, right, right_on, X_DOWN, X_UP, X - 1),
    ):
        g, h = [None] * 19, [None] * 19
        for n in range(5):
            g[pops[n]] = sent[n * Z : (n + 1) * Z, :]
            h[back[n]] = ref[n * Z : (n + 1) * Z, :]
        there = 3.0 * ref[X_RHO : X_RHO + Z, :]
        here = 3.0 * on * rho[x * Z : (x + 1) * Z, :]
        beyond.append(
            [
                there * (ref[X_MOM + d * Z : X_MOM + (d + 1) * Z, :] + mom)
                for d, mom in enumerate(first_moments(g))
            ]
        )
        added.append([here * mom for mom in first_moments(h)])
    for d in range(3):
        corner = []
        for k, (ref, on) in enumerate(((low, low_on), (high, high_on))):
            at, far = X_EDGE + 3 * k + d, X_FAR + 3 * k + d
            for mine, theirs in ((sent_left, left), (sent_right, right)):
                scale = 3.0 * theirs[X_EDGE + 6 + k : X_EDGE + 7 + k, :]
                corner.append(scale * (theirs[at : at + 1, :] + mine[far : far + 1, :]))
            for theirs, x, side_on in ((left, 0, left_on), (right, X - 1, right_on)):
                scale = 3.0 * on * side_on * row(ref, Z_RHO + x)
                corner.append(scale * theirs[far : far + 1, :])
        tiles = [beyond[0][d], beyond[1][d], added[0][d], added[1][d], jnp.concatenate(corner), zero]
        for t in range(0, 6, 2):
            put(split, d * rows + t * 8, jnp.concatenate(tiles[t : t + 2]))

    sub = sublanes()
    kind = sub & 3
    corner_x = jnp.where(kind == 0, -1, jnp.where(kind == 1, X, jnp.where(kind == 2, 0, X - 1)))
    bottom = sub < 4

    def chunk(c, carry):
        where = chunk_of(c)
        w = weights_of(weight, where)
        bx, bz = bases(cell, where)
        dz = sub - bz
        at_low, at_high = bottom & (bz == 0), (sub >= 4) & (bz == Z - 1)
        inner, corner = [], []
        for a in range(3):
            wa = w[3 * a : 3 * a + 3]
            inner.append(pick(dz, wa))
            corner.append(jnp.where(at_low, wa[0], jnp.where(at_high, wa[2], 0.0)))
        factors = [
            jnp.where(bx == 0, inner[0], 0.0),
            jnp.where(bx == X - 1, inner[2], 0.0),
            jnp.where(bx == 0, inner[1], jnp.where(bx == 1, inner[0], 0.0)),
            jnp.where(bx == X - 1, inner[1], jnp.where(bx == X - 2, inner[2], 0.0)),
            pick(corner_x - bx, corner),
        ]
        sums = []
        for d, tile in enumerate(gathered(split, rows, hot[:, where], factors)):
            sums.append(jnp.sum(acc_in[d, :, where] + tile, axis=0, keepdims=True))
            grad[d : d + 1, where] = sums[d]
        sums = jnp.concatenate(sums + [jnp.zeros((5, CHUNK), jnp.float32)])
        top = sums.astype(jnp.bfloat16)
        rest = (sums - top.astype(jnp.float32)).astype(jnp.bfloat16)
        totals[:, where] = jnp.concatenate([top, rest])
        return carry

    lax.fori_loop(0, cell.shape[1] // CHUNK, chunk, 0, unroll=UNROLL_C)
    total = lax.dot_general(
        totals[...], which[...], (((1,), (1,)), ((), ())), preferred_element_type=jnp.float32
    )
    result = total[0:3] + total[8:11]
    for n in range(partial.shape[0]):
        partial[n] = result


def ring(axis, step):
    count = lax.axis_size(axis)
    return [(i, (i + step) % count) for i in range(count)]


PARAMS = pltpu.CompilerParams(vmem_limit_bytes=48 * 1024 * 1024)


def cost(flops, moved):
    return pl.CostEstimate(flops=flops, bytes_accessed=moved, transcendentals=0)


def shape(*dims):
    return jax.ShapeDtypeStruct(dims, jnp.float32)


def pair(low):
    index = 0 if low else X // 2 - 1
    return pl.BlockSpec((19, 2, Z, Y), lambda i: (0, index, 0, 0))


def local(stored, adj, marker_cell, marker_weight, marker_panel, marker_count):
    slots = marker_cell.shape[0]
    whole = pl.BlockSpec(memory_space=pltpu.VMEM)
    hbm = pl.BlockSpec(memory_space=pltpu.HBM)
    any_space = pl.BlockSpec(memory_space=pl.ANY)
    cell, panel = marker_cell.reshape(1, slots), marker_panel.reshape(1, slots)
    to_low, to_high, mom, rho = pl.pallas_call(
        pack_z,
        out_shape=(
            shape(ZROWS, Y),
            shape(ZROWS, Y),
            shape(3, X * Z, Y),
            shape(X * Z, Y),
        ),
        in_specs=[hbm, hbm],
        out_specs=(whole,) * 4,
        scratch_shapes=[
            pltpu.VMEM(stored.shape, stored.dtype),
            pltpu.VMEM(adj.shape, adj.dtype),
            pltpu.SemaphoreType.DMA((2, GROUPS)),
        ],
        compiler_params=pltpu.CompilerParams(vmem_limit_bytes=52 * 1024 * 1024),
        cost_estimate=cost(5_000_000, 4_000_000),
    )(stored, adj)
    low = lax.ppermute(to_high, "gz", ring("gz", 1))
    high = lax.ppermute(to_low, "gz", ring("gz", -1))
    weight, hot, acc = pl.pallas_call(
        stage_a,
        out_shape=(
            shape(9, slots),
            jax.ShapeDtypeStruct((Y, slots), jnp.bfloat16),
            shape(3, 8, slots),
        ),
        in_specs=[pl.BlockSpec(memory_space=pltpu.SMEM)] + [whole] * 4,
        scratch_shapes=[pltpu.VMEM((6 * X * Z, Y), jnp.bfloat16)],
        compiler_params=PARAMS,
        cost_estimate=cost(800_000_000, 2_000_000),
    )(marker_count, mom, rho, cell, marker_weight)
    to_left, to_right = pl.pallas_call(
        pack_x,
        grid=(1,),
        out_shape=(shape(XROWS, Y), shape(XROWS, Y)),
        in_specs=[pair(True), pair(False), pair(True), pair(False)] + [whole] * 4 + [any_space],
        compiler_params=PARAMS,
        cost_estimate=cost(1_000_000, 2_000_000),
    )(stored, stored, adj, adj, to_low, to_high, low, high, acc)
    left = lax.ppermute(to_right, "gx", ring("gx", 1))
    right = lax.ppermute(to_left, "gx", ring("gx", -1))
    acc, which = pl.pallas_call(
        stage_b,
        out_shape=(shape(3, 8, slots), jax.ShapeDtypeStruct((PANELS, slots), jnp.bfloat16)),
        scratch_shapes=[pltpu.VMEM((24 * X, Y), jnp.bfloat16)],
        compiler_params=PARAMS,
        cost_estimate=cost(400_000_000, 2_000_000),
    )(to_low, to_high, low, high, cell, panel, weight, hot, acc)
    out = pl.pallas_call(
        interior,
        out_shape=shape(19, X, Z, Y),
        compiler_params=PARAMS,
        cost_estimate=cost(10_000_000, 7_000_000),
    )(stored, adj, low, high)
    grad, partial = pl.pallas_call(
        stage_c,
        out_shape=(shape(3, slots), shape(lax.axis_size("gz"), 3, PANELS)),
        scratch_shapes=[
            pltpu.VMEM((6 * 48, Y), jnp.bfloat16),
            pltpu.VMEM((16, slots), jnp.bfloat16),
        ],
        compiler_params=PARAMS,
        cost_estimate=cost(300_000_000, 2_000_000),
    )(rho, to_left, to_right, low, high, left, right, cell, weight, hot, which, acc)
    out = pl.pallas_call(
        borders,
        grid=(1,),
        out_shape=shape(19, X, Z, Y),
        in_specs=[pair(True), pair(False), pair(True), pair(False)] + [whole] * 4 + [any_space],
        out_specs=any_space,
        scratch_shapes=[
            pltpu.VMEM((2, 19, Z, Y), jnp.float32),
            pltpu.SemaphoreType.DMA((2,)),
        ],
        input_output_aliases={8: 0},
        compiler_params=PARAMS,
        cost_estimate=cost(1_000_000, 2_000_000),
    )(stored, stored, adj, adj, low, high, left, right, out)
    total = jnp.sum(lax.all_to_all(partial, "gz", 0, 0), axis=0)
    copies = jnp.broadcast_to(total[None], (lax.axis_size("gx"),) + total.shape)
    total = jnp.sum(lax.all_to_all(copies, "gx", 0, 0), axis=0)
    return (out, grad, total)


def solution(mesh):
    return jax.shard_map(
        local,
        mesh=mesh,
        in_specs=(
            P(None, "gx", "gz", None),
            P(None, "gx", "gz", None),
            P(("gx", "gz")),
            P(None, ("gx", "gz")),
            P(("gx", "gz")),
            P(("gx", "gz")),
        ),
        out_specs=(P(None, "gx", "gz", None), P(None, ("gx", "gz")), P()),
        check_vma=False,
    )
```

```python
import functools

import jax
import jax.numpy as jnp
from jax import lax
from jax.experimental import pallas as pl
from jax.experimental.pallas import tpu as pltpu
from jax.sharding import PartitionSpec as P

PANELS = 128
STENCIL = [
    (0, 0, 0),
    (1, 0, 0),
    (-1, 0, 0),
    (0, 1, 0),
    (0, -1, 0),
    (0, 0, 1),
    (0, 0, -1),
    (1, 1, 0),
    (-1, 1, 0),
    (1, -1, 0),
    (-1, -1, 0),
    (1, 0, 1),
    (-1, 0, 1),
    (1, 0, -1),
    (-1, 0, -1),
    (0, 1, 1),
    (0, -1, 1),
    (0, 1, -1),
    (0, -1, -1),
]
W0, W1, W2 = 1.0 / 3.0, 1.0 / 18.0, 1.0 / 36.0
WEIGHTS = [W0] + [W1] * 6 + [W2] * 12
OMEGA = 1.6

X, Z, Y = 16, 8, 256
X_UP = [q for q in range(19) if STENCIL[q][0] == 1]
X_DOWN = [q for q in range(19) if STENCIL[q][0] == -1]
Z_UP = [q for q in range(19) if STENCIL[q][2] == 1]
Z_DOWN = [q for q in range(19) if STENCIL[q][2] == -1]

ZROWS, Z_RHO, Z_MOM, Z_SPILL = 152, 80, 96, 144
XROWS, X_MOM, X_RHO, X_EDGE, X_FAR = 88, 40, 64, 72, 80

GX = ("y", "zh")
GZ = ("x", "zl", "core")
FIRST = ("core", "zh", "zl")
SECOND = ("y", "x")

CHUNK = 256
UNROLL_C = 8
GROUPS = 4
STEP = X // GROUPS
NEAR = (0, 1, X - 2, X - 1)


def roll_y(tile, q):
    step = STENCIL[q][1]
    if step == 0:
        return tile
    return pltpu.roll(tile, (-step) % Y, tile.ndim - 1)


def first_moments(g):
    def total(terms):
        out = None
        for q, sign in terms:
            if g[q] is None:
                continue
            if out is None:
                out = g[q] if sign > 0 else -g[q]
            else:
                out = out + g[q] if sign > 0 else out - g[q]
        return out

    parts = []
    for d in range(3):
        axis = total([(q, STENCIL[q][d]) for q in range(1, 7) if STENCIL[q][d]])
        diag = total([(q, STENCIL[q][d]) for q in range(7, 19) if STENCIL[q][d]])
        if axis is None and diag is None:
            parts.append(None)
        elif axis is None:
            parts.append(W2 * diag)
        elif diag is None:
            parts.append(W1 * axis)
        else:
            parts.append(W1 * axis + W2 * diag)
    return parts


def z_shift(tile, q, low, high):
    step = STENCIL[q][2]
    if step == 0:
        return tile
    rows = lax.broadcasted_iota(jnp.int32, tile.shape, 0)
    halo, edge = (high, Z - 1) if step > 0 else (low, 0)
    if halo is None:
        halo = jnp.zeros_like(tile)
    return jnp.where(rows == edge, halo, pltpu.roll(tile, (-step) % Z, 0))


def pulled_own(adj, q, x):
    return roll_y(z_shift(adj[q, x], q, None, None), q)


def row(ref, index):
    return ref[pl.ds(index, 1), :]


def pulled_z(adj, q, x, low, high, plane, low_on, high_on):
    step = STENCIL[q][2]
    lo = hi = None
    if step < 0:
        lo = row(low, Z_DOWN.index(q) * X + x) * low_on
    if step > 0:
        hi = row(high, Z_UP.index(q) * X + x) * high_on
    return roll_y(z_shift(adj[q, plane], q, lo, hi), q)


def ends():
    gz, gx = lax.axis_index(GZ), lax.axis_index(GX)
    gz_n, gx_n = lax.axis_size(GZ), lax.axis_size(GX)
    flag = lambda c: jnp.where(c, 1.0, 0.0).astype(jnp.float32)
    return flag(gz > 0), flag(gz < gz_n - 1), flag(gx > 0), flag(gx < gx_n - 1)


def column(adj, x):
    g = [None] * 19
    for q in range(1, 19):
        at = x + STENCIL[q][0]
        if 0 <= at < X:
            g[q] = pulled_own(adj, q, at)
    return first_moments(g)


def pack_z(stored_in, adj_in, to_low, to_high, rho_out, stored, adj, sems):
    copies = []
    for n in range(GROUPS):
        part = pl.ds(n * STEP, STEP)
        group = []
        for k, first in enumerate((0, Z - 2)):
            at = (pl.ds(1, 18), part, pl.ds(first, 2))
            group.append(pltpu.make_async_copy(adj_in.at[at], adj.at[at], sems.at[k, n]))
        group.append(
            pltpu.make_async_copy(stored_in.at[:, part], stored.at[:, part], sems.at[2, n])
        )
        for copy in group:
            copy.start()
        copies.append(group)

    def density(x):
        rho = stored[0, x].astype(jnp.float32)
        for q in range(1, 19):
            rho = rho + stored[q, x].astype(jnp.float32)
        rho_out[pl.ds(x * Z, Z), :] = rho
        to_low[pl.ds(Z_RHO + x, 1), :] = rho[0:1]
        to_high[pl.ds(Z_RHO + x, 1), :] = rho[Z - 1 : Z]
        for n in range(5):
            to_low[pl.ds(n * X + x, 1), :] = adj[Z_UP[n], x, 0:1, :]
            to_high[pl.ds(n * X + x, 1), :] = adj[Z_DOWN[n], x, Z - 1 : Z, :]

    def moments(x):
        for d, mom in enumerate(column(adj, x)):
            to_low[pl.ds(Z_MOM + d * X + x, 1), :] = mom[0:1]
            to_high[pl.ds(Z_MOM + d * X + x, 1), :] = mom[Z - 1 : Z]

    for n in range(GROUPS):
        for copy in copies[n]:
            copy.wait()
        first, last = n * STEP, (n + 1) * STEP
        for x in range(first, last):
            density(x)
        for x in range(max(first - 1, 0), last if n == GROUPS - 1 else last - 1):
            moments(x)
    spill = [column(adj, -1), column(adj, X)]
    zero = jnp.zeros((1, Y), jnp.float32)
    low_rows, high_rows = [], []
    for d in range(3):
        for side in range(2):
            mom = spill[side][d]
            low_rows.append(zero if mom is None else mom[0:1])
            high_rows.append(zero if mom is None else mom[Z - 1 : Z])
    to_low[Z_SPILL:, :] = jnp.concatenate(low_rows + [zero, zero])
    to_high[Z_SPILL:, :] = jnp.concatenate(high_rows + [zero, zero])


def shift_rows(tile, step):
    if step == 0:
        return tile
    rows = lax.broadcasted_iota(jnp.int32, tile.shape, 0)
    edge = X - 1 if step > 0 else 0
    return jnp.where(rows == edge, 0.0, pltpu.roll(tile, (-step) % X, 0))


def edge_moments(sent, pops):
    tiles, before, after = [None] * 19, [None] * 19, [None] * 19
    for n, q in enumerate(pops):
        tile = roll_y(sent[n * X : (n + 1) * X, :], q)
        step = STENCIL[q][0]
        tiles[q] = shift_rows(tile, step)
        if step > 0:
            before[q] = tile[0:1]
        if step < 0:
            after[q] = tile[X - 1 : X]
    return first_moments(tiles), first_moments(before), first_moments(after)


def plus(a, b):
    return a if b is None else a + b


def pack_x(near, rho, sent_low, sent_high, low, high, after, to_left, to_right):
    del after
    low_on, high_on, _, _ = ends()
    edge_low, edge_high = edge_moments(sent_low, Z_UP), edge_moments(sent_high, Z_DOWN)

    def side(out, x, plane, inner, away, skip):
        for n, q in enumerate(away):
            out[n * Z : (n + 1) * Z, :] = pulled_z(
                near, q, x, low, high, plane, low_on, high_on
            )
        g = [None] * 19
        for q in range(1, 19):
            step = STENCIL[q][0]
            if step == 0:
                g[q] = pulled_z(near, q, x, low, high, plane, low_on, high_on)
            elif step != skip:
                g[q] = pulled_z(near, q, x + step, low, high, inner, low_on, high_on)
        for d, mom in enumerate(first_moments(g)):
            out[X_MOM + d * Z : X_MOM + (d + 1) * Z, :] = mom
        out[X_RHO : X_RHO + Z, :] = rho[x * Z : (x + 1) * Z, :]
        beyond = 1 if x > 0 else 0
        edge, far = [], []
        for ref, own, on in ((low, edge_low, low_on), (high, edge_high, high_on)):
            for d in range(3):
                here = row(ref, Z_MOM + d * X + x) * on
                edge.append(here + own[0][d][x : x + 1])
                there = row(ref, Z_SPILL + 2 * d + beyond) * on
                far.append(plus(there, own[1 + beyond][d]))
        for ref, on in ((low, low_on), (high, high_on)):
            edge.append(row(ref, Z_RHO + x) * on)
        out[X_EDGE : X_EDGE + 8, :] = jnp.concatenate(edge)
        far = far + [jnp.zeros((1, Y), jnp.float32)] * 2
        out[X_FAR : X_FAR + 8, :] = jnp.concatenate(far)

    side(to_left, 0, 0, 1, X_UP, -1)
    side(to_right, X - 1, 3, 2, X_DOWN, 1)


def collide_transpose(f, g, emit):
    rho = f[0]
    for q in range(1, 19):
        rho = rho + f[q]
    jx = (f[1] - f[2]) + (f[7] - f[8]) + (f[9] - f[10]) + (f[11] - f[12]) + (f[13] - f[14])
    jy = (f[3] - f[4]) + (f[7] - f[9]) + (f[8] - f[10]) + (f[15] - f[16]) + (f[17] - f[18])
    jz = (f[5] - f[6]) + (f[11] - f[13]) + (f[12] - f[14]) + (f[15] - f[17]) + (f[16] - f[18])
    inv = 1.0 / rho
    ux, uy, uz = jx * inv, jy * inv, jz * inv

    sx, sy, sz = W1 * (g[1] + g[2]), W1 * (g[3] + g[4]), W1 * (g[5] + g[6])
    dx, dy, dz = W1 * (g[1] - g[2]), W1 * (g[3] - g[4]), W1 * (g[5] - g[6])

    def plane(a, b, c, d):
        p, m = g[a] + g[d], g[b] + g[c]
        r, s = g[a] - g[d], g[b] - g[c]
        return W2 * (p + m), W2 * (p - m), W2 * (r - s), W2 * (r + s)

    s_xy, c_xy, xy_x, xy_y = plane(7, 8, 9, 10)
    s_xz, c_xz, xz_x, xz_z = plane(11, 12, 13, 14)
    s_yz, c_yz, yz_y, yz_z = plane(15, 16, 17, 18)
    m_x = dx + xy_x + xz_x
    m_y = dy + xy_y + yz_y
    m_z = dz + xz_z + yz_z
    g_xx = sx + s_xy + s_xz
    g_yy = sy + s_xy + s_yz
    g_zz = sz + s_xz + s_yz
    g0 = W0 * g[0] + (sx + sy + sz) + (s_xy + s_xz + s_yz)
    vx = g_xx * ux + c_xy * uy + c_xz * uz
    vy = c_xy * ux + g_yy * uy + c_yz * uz
    vz = c_xz * ux + c_yz * uy + g_zz * uz
    uv = ux * vx + uy * vy + uz * vz
    uu = ux * ux + uy * uy + uz * uz
    base = OMEGA * (g0 - 4.5 * uv + 1.5 * uu * g0)
    bx = OMEGA * (3.0 * m_x + 9.0 * vx - 3.0 * ux * g0)
    by = OMEGA * (3.0 * m_y + 9.0 * vy - 3.0 * uy * g0)
    bz = OMEGA * (3.0 * m_z + 9.0 * vz - 3.0 * uz * g0)
    xp, xm = base + bx, base - bx
    yp, ym = base + by, base - by
    along = {
        (0, 0, 0): base,
        (1, 0, 0): xp,
        (-1, 0, 0): xm,
        (0, 1, 0): yp,
        (0, -1, 0): ym,
        (0, 0, 1): base + bz,
        (0, 0, -1): base - bz,
        (1, 1, 0): xp + by,
        (-1, 1, 0): xm + by,
        (1, -1, 0): xp - by,
        (-1, -1, 0): xm - by,
        (1, 0, 1): xp + bz,
        (-1, 0, 1): xm + bz,
        (1, 0, -1): xp - bz,
        (-1, 0, -1): xm - bz,
        (0, 1, 1): yp + bz,
        (0, -1, 1): ym + bz,
        (0, 1, -1): yp - bz,
        (0, -1, -1): ym - bz,
    }
    for q in range(19):
        emit(q, along[STENCIL[q]] + (1.0 - OMEGA) * g[q])


def output(
    stored_in,
    adj_in,
    low,
    high,
    left,
    right,
    grad,
    out_hbm,
    grad_hbm,
    stored,
    adj,
    out,
    in_sems,
    out_sems,
):
    low_on, high_on, left_on, right_on = ends()
    reads, writes = [], []
    for n in range(GROUPS):
        part = pl.ds(n * STEP, STEP)
        for k, (src, dst) in enumerate(((adj_in, adj), (stored_in, stored))):
            copy = pltpu.make_async_copy(src.at[:, part], dst.at[:, part], in_sems.at[k, n])
            copy.start()
            reads.append(copy)
    copy = pltpu.make_async_copy(grad, grad_hbm, out_sems.at[GROUPS])
    copy.start()
    writes.append(copy)

    def plane(x, taken=(), ref=None, on=None):
        f = [stored[q, x].astype(jnp.float32) for q in range(19)]
        g = []
        for q in range(19):
            at = x + STENCIL[q][0]
            if q in taken:
                n = taken.index(q)
                g.append(ref[n * Z : (n + 1) * Z, :] * on)
            else:
                g.append(pulled_z(adj, q, at, low, high, at, low_on, high_on))

        def emit(q, value):
            out[q, x] = value

        collide_transpose(f, g, emit)

    def body(x, carry):
        plane(x)
        return carry

    done = 0
    for n in range(GROUPS):
        reads[2 * n].wait()
        reads[2 * n + 1].wait()
        ready = (n + 1) * STEP - 1
        if n == 0:
            plane(0, X_DOWN, left, left_on)
        lax.fori_loop(max(done, 1), ready, body, 0)
        if n == GROUPS - 1:
            plane(X - 1, X_UP, right, right_on)
            ready = X
        part = pl.ds(done, ready - done)
        copy = pltpu.make_async_copy(out.at[:, part], out_hbm.at[:, part], out_sems.at[n])
        copy.start()
        writes.append(copy)
        done = ready
    for copy in writes:
        copy.wait()


def put(split, at, tile):
    head = tile.astype(jnp.bfloat16)
    split[pl.ds(at, tile.shape[0]), :] = head
    rest = (tile - head.astype(jnp.float32)).astype(jnp.bfloat16)
    split[pl.ds(split.shape[0] // 2 + at, tile.shape[0]), :] = rest


def bases(cell, where):
    cells = cell[:, where]
    bx = jnp.broadcast_to(cells >> 11, (8, CHUNK))
    bz = jnp.broadcast_to((cells >> 8) & 7, (8, CHUNK))
    return bx, bz


def pick(dx, three):
    return jnp.where(
        dx == -1, three[0], jnp.where(dx == 0, three[1], jnp.where(dx == 1, three[2], 0.0))
    )


def gathered(split, rows, hot, factors):
    picked = jnp.dot(split[...], hot, preferred_element_type=jnp.float32)
    half = split.shape[0] // 2
    out = []
    for d in range(3):
        summed = None
        for t, factor in enumerate(factors):
            at = d * rows + 8 * t
            term = factor * (picked[at : at + 8] + picked[half + at : half + at + 8])
            summed = term if summed is None else summed + term
        out.append(summed)
    return out


def sublanes():
    return lax.broadcasted_iota(jnp.int32, (8, CHUNK), 0)


def chunk_of(c):
    return pl.ds(pl.multiple_of(c * CHUNK, CHUNK), CHUNK)


def weights_of(weight, where):
    return [jnp.broadcast_to(weight[s : s + 1, where], (8, CHUNK)) for s in range(9)]


def stage_a(count, adj, rho, cell, weight, live_weight, hot, acc, near, split):
    rows = X * Z
    for k, x in enumerate(NEAR):
        near[:, k] = adj[:, x]
    for x in range(0, X, 2):
        scale = 3.0 * rho[x * Z : (x + 2) * Z, :]
        first, second = column(adj, x), column(adj, x + 1)
        for d in range(3):
            put(split, d * rows + x * Z, scale * jnp.concatenate([first[d], second[d]]))
    lanes = lax.broadcasted_iota(jnp.int32, (9, CHUNK), 1)

    def chunk(c, carry):
        where = chunk_of(c)
        live = (lanes + c * CHUNK) < count[0]
        live_weight[:, where] = jnp.where(live, weight[:, where], 0.0)
        w = weights_of(live_weight, where)
        y_of = jnp.broadcast_to(cell[:, where] & (Y - 1), (Y, CHUNK))
        one = jnp.where(lax.broadcasted_iota(jnp.int32, (Y, CHUNK), 0) == y_of, 1.0, 0.0)
        one = one.astype(jnp.bfloat16)
        hot[:, where] = one
        bx, bz = bases(cell, where)
        dz = sublanes() - bz
        three = [pick(dz, w[3 * a : 3 * a + 3]) for a in range(3)]
        factors = [pick(x - bx, three) for x in range(X)]
        for d, tile in enumerate(gathered(split, rows, one, factors)):
            acc[d, :, where] = tile
        return carry

    lax.fori_loop(0, cell.shape[1] // CHUNK, chunk, 0, unroll=4)


def stage_b(
    sent_low, sent_high, low, high, cell, panel, weight, hot, acc_in, acc, which, split
):
    low_on, high_on, _, _ = ends()
    rows = 4 * X
    for k, (sent, up, back, ref, on) in enumerate(
        (
            (sent_low, Z_UP, Z_DOWN, low, low_on),
            (sent_high, Z_DOWN, Z_UP, high, high_on),
        )
    ):
        beyond, _, _ = edge_moments(sent, up)
        added, _, _ = edge_moments(ref, back)
        here = 3.0 * sent[Z_RHO : Z_RHO + X, :] * on
        there = 3.0 * ref[Z_RHO : Z_RHO + X, :]
        for d in range(3):
            put(split, d * rows + k * X, here * added[d])
            mom = beyond[d] + ref[Z_MOM + d * X : Z_MOM + (d + 1) * X, :]
            put(split, d * rows + (2 + k) * X, there * mom)

    def chunk(c, carry):
        where = chunk_of(c)
        w = weights_of(weight, where)
        bx, bz = bases(cell, where)
        sub = sublanes()
        dx = [sub - bx, sub + 8 - bx]
        first, last, under, over = [], [], [], []
        for a in range(3):
            wa = w[3 * a : 3 * a + 3]
            first.append(jnp.where(bz == 0, wa[1], jnp.where(bz == 1, wa[0], 0.0)))
            last.append(jnp.where(bz == Z - 1, wa[1], jnp.where(bz == Z - 2, wa[2], 0.0)))
            under.append(jnp.where(bz == 0, wa[0], 0.0))
            over.append(jnp.where(bz == Z - 1, wa[2], 0.0))
        factors = [pick(at, three) for three in (first, last, under, over) for at in dx]
        for d, tile in enumerate(gathered(split, rows, hot[:, where], factors)):
            acc[d, :, where] = acc_in[d, :, where] + tile
        panels = jnp.broadcast_to(panel[:, where], (PANELS, CHUNK))
        match = lax.broadcasted_iota(jnp.int32, (PANELS, CHUNK), 0) == panels
        which[:, where] = jnp.where(match, 1.0, 0.0).astype(jnp.bfloat16)
        return carry

    lax.fori_loop(0, cell.shape[1] // CHUNK, chunk, 0, unroll=4)


def stage_c(
    rho,
    sent_left,
    sent_right,
    low,
    high,
    left,
    right,
    cell,
    weight,
    hot,
    which,
    acc_in,
    grad,
    partial,
    split,
    totals,
):
    low_on, high_on, left_on, right_on = ends()
    rows = 48
    zero = jnp.zeros((8, Y), jnp.float32)
    beyond, added = [], []
    for sent, ref, on, pops, back, x in (
        (sent_left, left, left_on, X_UP, X_DOWN, 0),
        (sent_right, right, right_on, X_DOWN, X_UP, X - 1),
    ):
        g, h = [None] * 19, [None] * 19
        for n in range(5):
            g[pops[n]] = sent[n * Z : (n + 1) * Z, :]
            h[back[n]] = ref[n * Z : (n + 1) * Z, :]
        there = 3.0 * ref[X_RHO : X_RHO + Z, :]
        here = 3.0 * on * rho[x * Z : (x + 1) * Z, :]
        beyond.append(
            [
                there * (ref[X_MOM + d * Z : X_MOM + (d + 1) * Z, :] + mom)
                for d, mom in enumerate(first_moments(g))
            ]
        )
        added.append([here * mom for mom in first_moments(h)])
    for d in range(3):
        corner = []
        for k, (ref, on) in enumerate(((low, low_on), (high, high_on))):
            at, far = X_EDGE + 3 * k + d, X_FAR + 3 * k + d
            for mine, theirs in ((sent_left, left), (sent_right, right)):
                scale = 3.0 * theirs[X_EDGE + 6 + k : X_EDGE + 7 + k, :]
                corner.append(scale * (theirs[at : at + 1, :] + mine[far : far + 1, :]))
            for theirs, x, side_on in ((left, 0, left_on), (right, X - 1, right_on)):
                scale = 3.0 * on * side_on * row(ref, Z_RHO + x)
                corner.append(scale * theirs[far : far + 1, :])
        tiles = [beyond[0][d], beyond[1][d], added[0][d], added[1][d], jnp.concatenate(corner), zero]
        for t in range(0, 6, 2):
            put(split, d * rows + t * 8, jnp.concatenate(tiles[t : t + 2]))

    sub = sublanes()
    kind = sub & 3
    corner_x = jnp.where(kind == 0, -1, jnp.where(kind == 1, X, jnp.where(kind == 2, 0, X - 1)))
    bottom = sub < 4

    def chunk(c, carry):
        where = chunk_of(c)
        w = weights_of(weight, where)
        bx, bz = bases(cell, where)
        dz = sub - bz
        at_low, at_high = bottom & (bz == 0), (sub >= 4) & (bz == Z - 1)
        inner, corner = [], []
        for a in range(3):
            wa = w[3 * a : 3 * a + 3]
            inner.append(pick(dz, wa))
            corner.append(jnp.where(at_low, wa[0], jnp.where(at_high, wa[2], 0.0)))
        factors = [
            jnp.where(bx == 0, inner[0], 0.0),
            jnp.where(bx == X - 1, inner[2], 0.0),
            jnp.where(bx == 0, inner[1], jnp.where(bx == 1, inner[0], 0.0)),
            jnp.where(bx == X - 1, inner[1], jnp.where(bx == X - 2, inner[2], 0.0)),
            pick(corner_x - bx, corner),
        ]
        sums = []
        for d, tile in enumerate(gathered(split, rows, hot[:, where], factors)):
            sums.append(jnp.sum(acc_in[d, :, where] + tile, axis=0, keepdims=True))
            grad[d : d + 1, where] = sums[d]
        sums = jnp.concatenate(sums + [jnp.zeros((5, CHUNK), jnp.float32)])
        top = sums.astype(jnp.bfloat16)
        rest = (sums - top.astype(jnp.float32)).astype(jnp.bfloat16)
        totals[:, where] = jnp.concatenate([top, rest])
        return carry

    lax.fori_loop(0, cell.shape[1] // CHUNK, chunk, 0, unroll=UNROLL_C)
    total = lax.dot_general(
        totals[...], which[...], (((1,), (1,)), ((), ())), preferred_element_type=jnp.float32
    )
    result = total[0:3] + total[8:11]
    for n in range(partial.shape[0]):
        partial[n] = result


def ring(axis, step):
    count = lax.axis_size(axis)
    return [(i, (i + step) % count) for i in range(count)]


PARAMS = pltpu.CompilerParams(vmem_limit_bytes=48 * 1024 * 1024)
FIRST_BIG = pltpu.CompilerParams(vmem_limit_bytes=53 * 1024 * 1024)
BIG = pltpu.CompilerParams(vmem_limit_bytes=52 * 1024 * 1024)


def cost(flops, moved):
    return pl.CostEstimate(flops=flops, bytes_accessed=moved, transcendentals=0)


def shape(*dims):
    return jax.ShapeDtypeStruct(dims, jnp.float32)


def summed(parts, count):
    total = jnp.sum(parts, axis=0)
    return jnp.broadcast_to(total[None], (count,) + total.shape)


def local(stored, adj, marker_cell, marker_weight, marker_panel, marker_count):
    slots = marker_cell.shape[0]
    whole = pl.BlockSpec(memory_space=pltpu.VMEM)
    hbm = pl.BlockSpec(memory_space=pltpu.HBM)
    any_space = pl.BlockSpec(memory_space=pl.ANY)
    cell, panel = marker_cell.reshape(1, slots), marker_panel.reshape(1, slots)
    to_low, to_high, rho = pl.pallas_call(
        pack_z,
        out_shape=(
            shape(ZROWS, Y),
            shape(ZROWS, Y),
            shape(X * Z, Y),
        ),
        in_specs=[hbm, hbm],
        out_specs=(whole,) * 3,
        scratch_shapes=[
            pltpu.VMEM(stored.shape, stored.dtype),
            pltpu.VMEM(adj.shape, adj.dtype),
            pltpu.SemaphoreType.DMA((3, GROUPS)),
        ],
        compiler_params=FIRST_BIG,
        cost_estimate=cost(5_000_000, 4_000_000),
    )(stored, adj)
    low = lax.ppermute(to_high, GZ, ring(GZ, 1))
    high = lax.ppermute(to_low, GZ, ring(GZ, -1))
    weight, hot, acc, near = pl.pallas_call(
        stage_a,
        out_shape=(
            shape(9, slots),
            jax.ShapeDtypeStruct((Y, slots), jnp.bfloat16),
            shape(3, 8, slots),
            shape(19, len(NEAR), Z, Y),
        ),
        in_specs=[pl.BlockSpec(memory_space=pltpu.SMEM)] + [whole] * 4,
        scratch_shapes=[pltpu.VMEM((6 * X * Z, Y), jnp.bfloat16)],
        compiler_params=PARAMS,
        cost_estimate=cost(800_000_000, 2_000_000),
    )(marker_count, adj, rho, cell, marker_weight)
    to_left, to_right = pl.pallas_call(
        pack_x,
        out_shape=(shape(XROWS, Y), shape(XROWS, Y)),
        in_specs=[whole] * 6 + [any_space],
        compiler_params=PARAMS,
        cost_estimate=cost(1_000_000, 2_000_000),
    )(near, rho, to_low, to_high, low, high, acc)
    left = lax.ppermute(to_right, GX, ring(GX, 1))
    right = lax.ppermute(to_left, GX, ring(GX, -1))
    acc, which = pl.pallas_call(
        stage_b,
        out_shape=(shape(3, 8, slots), jax.ShapeDtypeStruct((PANELS, slots), jnp.bfloat16)),
        scratch_shapes=[pltpu.VMEM((24 * X, Y), jnp.bfloat16)],
        compiler_params=PARAMS,
        cost_estimate=cost(400_000_000, 2_000_000),
    )(to_low, to_high, low, high, cell, panel, weight, hot, acc)
    grad, partial = pl.pallas_call(
        stage_c,
        out_shape=(shape(3, slots), shape(lax.axis_size(FIRST), 3, PANELS)),
        scratch_shapes=[
            pltpu.VMEM((6 * 48, Y), jnp.bfloat16),
            pltpu.VMEM((16, slots), jnp.bfloat16),
        ],
        compiler_params=PARAMS,
        cost_estimate=cost(300_000_000, 2_000_000),
    )(rho, to_left, to_right, low, high, left, right, cell, weight, hot, which, acc)
    out, grad = pl.pallas_call(
        output,
        out_shape=(shape(19, X, Z, Y), shape(3, slots)),
        in_specs=[hbm, hbm] + [whole] * 5,
        out_specs=(hbm, hbm),
        scratch_shapes=[
            pltpu.VMEM(stored.shape, stored.dtype),
            pltpu.VMEM(adj.shape, adj.dtype),
            pltpu.VMEM(adj.shape, adj.dtype),
            pltpu.SemaphoreType.DMA((2, GROUPS)),
            pltpu.SemaphoreType.DMA((GROUPS + 1,)),
        ],
        compiler_params=BIG,
        cost_estimate=cost(10_000_000, 7_000_000),
    )(stored, adj, low, high, left, right, grad)
    partial = summed(lax.all_to_all(partial, FIRST, 0, 0), lax.axis_size(SECOND))
    total = jnp.sum(lax.all_to_all(partial, SECOND, 0, 0), axis=0)
    return (out, grad, total)


def solution(mesh):
    split = jax.sharding.Mesh(
        mesh.devices.reshape(4, 4, 4, 2, 2), ("y", "zh", "x", "zl", "core")
    )
    return jax.shard_map(
        local,
        mesh=split,
        in_specs=(
            P(None, GX, GZ, None),
            P(None, GX, GZ, None),
            P(GX + GZ),
            P(None, GX + GZ),
            P(GX + GZ),
            P(GX + GZ),
        ),
        out_specs=(P(None, GX, GZ, None), P(None, GX + GZ), P()),
        check_vma=False,
    )
```

```python
import functools

import jax
import jax.numpy as jnp
from jax import lax
from jax.experimental import pallas as pl
from jax.experimental.pallas import tpu as pltpu
from jax.sharding import PartitionSpec as P

PANELS = 128
STENCIL = [
    (0, 0, 0),
    (1, 0, 0),
    (-1, 0, 0),
    (0, 1, 0),
    (0, -1, 0),
    (0, 0, 1),
    (0, 0, -1),
    (1, 1, 0),
    (-1, 1, 0),
    (1, -1, 0),
    (-1, -1, 0),
    (1, 0, 1),
    (-1, 0, 1),
    (1, 0, -1),
    (-1, 0, -1),
    (0, 1, 1),
    (0, -1, 1),
    (0, 1, -1),
    (0, -1, -1),
]
W0, W1, W2 = 1.0 / 3.0, 1.0 / 18.0, 1.0 / 36.0
WEIGHTS = [W0] + [W1] * 6 + [W2] * 12
OMEGA = 1.6

X, Z, Y = 16, 8, 256
X_UP = [q for q in range(19) if STENCIL[q][0] == 1]
X_DOWN = [q for q in range(19) if STENCIL[q][0] == -1]
Z_UP = [q for q in range(19) if STENCIL[q][2] == 1]
Z_DOWN = [q for q in range(19) if STENCIL[q][2] == -1]

ZROWS, Z_RHO, Z_MOM, Z_SPILL = 152, 80, 96, 144
XROWS, X_MOM, X_RHO, X_EDGE, X_FAR = 88, 40, 64, 72, 80

GX = ("y", "zh")
GZ = ("x", "zl", "core")
FIRST = ("core", "zh", "zl")
SECOND = ("y", "x")

CHUNK = 256
UNROLL_C = 8
GROUPS = 4
STEP = X // GROUPS
NEAR = (0, 1, X - 2, X - 1)


def roll_y(tile, q):
    step = STENCIL[q][1]
    if step == 0:
        return tile
    return pltpu.roll(tile, (-step) % Y, tile.ndim - 1)


def first_moments(g):
    def total(terms):
        out = None
        for q, sign in terms:
            if g[q] is None:
                continue
            if out is None:
                out = g[q] if sign > 0 else -g[q]
            else:
                out = out + g[q] if sign > 0 else out - g[q]
        return out

    parts = []
    for d in range(3):
        axis = total([(q, STENCIL[q][d]) for q in range(1, 7) if STENCIL[q][d]])
        diag = total([(q, STENCIL[q][d]) for q in range(7, 19) if STENCIL[q][d]])
        if axis is None and diag is None:
            parts.append(None)
        elif axis is None:
            parts.append(W2 * diag)
        elif diag is None:
            parts.append(W1 * axis)
        else:
            parts.append(W1 * axis + W2 * diag)
    return parts


def z_shift(tile, q, low, high):
    step = STENCIL[q][2]
    if step == 0:
        return tile
    rows = lax.broadcasted_iota(jnp.int32, tile.shape, 0)
    halo, edge = (high, Z - 1) if step > 0 else (low, 0)
    if halo is None:
        halo = jnp.zeros_like(tile)
    return jnp.where(rows == edge, halo, pltpu.roll(tile, (-step) % Z, 0))


def pulled_own(adj, q, x):
    return roll_y(z_shift(adj[q, x], q, None, None), q)


def row(ref, index):
    return ref[pl.ds(index, 1), :]


def pulled_z(adj, q, x, low, high, plane, low_on, high_on):
    step = STENCIL[q][2]
    lo = hi = None
    if step < 0:
        lo = row(low, Z_DOWN.index(q) * X + x) * low_on
    if step > 0:
        hi = row(high, Z_UP.index(q) * X + x) * high_on
    return roll_y(z_shift(adj[q, plane], q, lo, hi), q)


def ends():
    gz, gx = lax.axis_index(GZ), lax.axis_index(GX)
    gz_n, gx_n = lax.axis_size(GZ), lax.axis_size(GX)
    flag = lambda c: jnp.where(c, 1.0, 0.0).astype(jnp.float32)
    return flag(gz > 0), flag(gz < gz_n - 1), flag(gx > 0), flag(gx < gx_n - 1)


def column(adj, x):
    g = [None] * 19
    for q in range(1, 19):
        at = x + STENCIL[q][0]
        if 0 <= at < X:
            g[q] = pulled_own(adj, q, at)
    return first_moments(g)


def by_parity(index, first, second, even_first, even_second):
    even = lax.rem(index, 2) == 0
    a, b = even_first[...], even_second[...]
    first[...] = jnp.where(even, a, b)
    second[...] = jnp.where(even, b, a)


def pack_z(stored_in, adj_in, to_low, to_high, across, along, rho_out, stored, adj, sems):
    copies = []
    for n in range(GROUPS):
        part = pl.ds(n * STEP, STEP)
        group = []
        for k, first in enumerate((0, Z - 2)):
            at = (pl.ds(1, 18), part, pl.ds(first, 2))
            group.append(pltpu.make_async_copy(adj_in.at[at], adj.at[at], sems.at[k, n]))
        group.append(
            pltpu.make_async_copy(stored_in.at[:, part], stored.at[:, part], sems.at[2, n])
        )
        for copy in group:
            copy.start()
        copies.append(group)

    def density(x):
        rho = stored[0, x].astype(jnp.float32)
        for q in range(1, 19):
            rho = rho + stored[q, x].astype(jnp.float32)
        rho_out[pl.ds(x * Z, Z), :] = rho
        to_low[pl.ds(Z_RHO + x, 1), :] = rho[0:1]
        to_high[pl.ds(Z_RHO + x, 1), :] = rho[Z - 1 : Z]
        for n in range(5):
            to_low[pl.ds(n * X + x, 1), :] = adj[Z_UP[n], x, 0:1, :]
            to_high[pl.ds(n * X + x, 1), :] = adj[Z_DOWN[n], x, Z - 1 : Z, :]

    def moments(x):
        for d, mom in enumerate(column(adj, x)):
            to_low[pl.ds(Z_MOM + d * X + x, 1), :] = mom[0:1]
            to_high[pl.ds(Z_MOM + d * X + x, 1), :] = mom[Z - 1 : Z]

    for n in range(GROUPS):
        for copy in copies[n]:
            copy.wait()
        first, last = n * STEP, (n + 1) * STEP
        for x in range(first, last):
            density(x)
        for x in range(max(first - 1, 0), last if n == GROUPS - 1 else last - 1):
            moments(x)
    spill = [column(adj, -1), column(adj, X)]
    zero = jnp.zeros((1, Y), jnp.float32)
    low_rows, high_rows = [], []
    for d in range(3):
        for side in range(2):
            mom = spill[side][d]
            low_rows.append(zero if mom is None else mom[0:1])
            high_rows.append(zero if mom is None else mom[Z - 1 : Z])
    to_low[Z_SPILL:, :] = jnp.concatenate(low_rows + [zero, zero])
    to_high[Z_SPILL:, :] = jnp.concatenate(high_rows + [zero, zero])
    by_parity(lax.axis_index(GZ), across, along, to_high, to_low)


def shift_rows(tile, step):
    if step == 0:
        return tile
    rows = lax.broadcasted_iota(jnp.int32, tile.shape, 0)
    edge = X - 1 if step > 0 else 0
    return jnp.where(rows == edge, 0.0, pltpu.roll(tile, (-step) % X, 0))


def edge_moments(sent, pops):
    tiles, before, after = [None] * 19, [None] * 19, [None] * 19
    for n, q in enumerate(pops):
        tile = roll_y(sent[n * X : (n + 1) * X, :], q)
        step = STENCIL[q][0]
        tiles[q] = shift_rows(tile, step)
        if step > 0:
            before[q] = tile[0:1]
        if step < 0:
            after[q] = tile[X - 1 : X]
    return first_moments(tiles), first_moments(before), first_moments(after)


def plus(a, b):
    return a if b is None else a + b


def pack_x(
    near,
    rho,
    sent_low,
    sent_high,
    along_in,
    across_in,
    after,
    to_left,
    to_right,
    across,
    along,
    low,
    high,
):
    del after
    by_parity(lax.axis_index(GZ), high, low, across_in, along_in)
    low_on, high_on, _, _ = ends()
    edge_low, edge_high = edge_moments(sent_low, Z_UP), edge_moments(sent_high, Z_DOWN)

    def side(out, x, plane, inner, away, skip):
        for n, q in enumerate(away):
            out[n * Z : (n + 1) * Z, :] = pulled_z(
                near, q, x, low, high, plane, low_on, high_on
            )
        g = [None] * 19
        for q in range(1, 19):
            step = STENCIL[q][0]
            if step == 0:
                g[q] = pulled_z(near, q, x, low, high, plane, low_on, high_on)
            elif step != skip:
                g[q] = pulled_z(near, q, x + step, low, high, inner, low_on, high_on)
        for d, mom in enumerate(first_moments(g)):
            out[X_MOM + d * Z : X_MOM + (d + 1) * Z, :] = mom
        out[X_RHO : X_RHO + Z, :] = rho[x * Z : (x + 1) * Z, :]
        beyond = 1 if x > 0 else 0
        edge, far = [], []
        for ref, own, on in ((low, edge_low, low_on), (high, edge_high, high_on)):
            for d in range(3):
                here = row(ref, Z_MOM + d * X + x) * on
                edge.append(here + own[0][d][x : x + 1])
                there = row(ref, Z_SPILL + 2 * d + beyond) * on
                far.append(plus(there, own[1 + beyond][d]))
        for ref, on in ((low, low_on), (high, high_on)):
            edge.append(row(ref, Z_RHO + x) * on)
        out[X_EDGE : X_EDGE + 8, :] = jnp.concatenate(edge)
        far = far + [jnp.zeros((1, Y), jnp.float32)] * 2
        out[X_FAR : X_FAR + 8, :] = jnp.concatenate(far)

    side(to_left, 0, 0, 1, X_UP, -1)
    side(to_right, X - 1, 3, 2, X_DOWN, 1)
    by_parity(lax.axis_index(GX), across, along, to_right, to_left)


def collide_transpose(f, g, emit):
    rho = f[0]
    for q in range(1, 19):
        rho = rho + f[q]
    jx = (f[1] - f[2]) + (f[7] - f[8]) + (f[9] - f[10]) + (f[11] - f[12]) + (f[13] - f[14])
    jy = (f[3] - f[4]) + (f[7] - f[9]) + (f[8] - f[10]) + (f[15] - f[16]) + (f[17] - f[18])
    jz = (f[5] - f[6]) + (f[11] - f[13]) + (f[12] - f[14]) + (f[15] - f[17]) + (f[16] - f[18])
    inv = 1.0 / rho
    ux, uy, uz = jx * inv, jy * inv, jz * inv

    sx, sy, sz = W1 * (g[1] + g[2]), W1 * (g[3] + g[4]), W1 * (g[5] + g[6])
    dx, dy, dz = W1 * (g[1] - g[2]), W1 * (g[3] - g[4]), W1 * (g[5] - g[6])

    def plane(a, b, c, d):
        p, m = g[a] + g[d], g[b] + g[c]
        r, s = g[a] - g[d], g[b] - g[c]
        return W2 * (p + m), W2 * (p - m), W2 * (r - s), W2 * (r + s)

    s_xy, c_xy, xy_x, xy_y = plane(7, 8, 9, 10)
    s_xz, c_xz, xz_x, xz_z = plane(11, 12, 13, 14)
    s_yz, c_yz, yz_y, yz_z = plane(15, 16, 17, 18)
    m_x = dx + xy_x + xz_x
    m_y = dy + xy_y + yz_y
    m_z = dz + xz_z + yz_z
    g_xx = sx + s_xy + s_xz
    g_yy = sy + s_xy + s_yz
    g_zz = sz + s_xz + s_yz
    g0 = W0 * g[0] + (sx + sy + sz) + (s_xy + s_xz + s_yz)
    vx = g_xx * ux + c_xy * uy + c_xz * uz
    vy = c_xy * ux + g_yy * uy + c_yz * uz
    vz = c_xz * ux + c_yz * uy + g_zz * uz
    uv = ux * vx + uy * vy + uz * vz
    uu = ux * ux + uy * uy + uz * uz
    base = OMEGA * (g0 - 4.5 * uv + 1.5 * uu * g0)
    bx = OMEGA * (3.0 * m_x + 9.0 * vx - 3.0 * ux * g0)
    by = OMEGA * (3.0 * m_y + 9.0 * vy - 3.0 * uy * g0)
    bz = OMEGA * (3.0 * m_z + 9.0 * vz - 3.0 * uz * g0)
    xp, xm = base + bx, base - bx
    yp, ym = base + by, base - by
    along = {
        (0, 0, 0): base,
        (1, 0, 0): xp,
        (-1, 0, 0): xm,
        (0, 1, 0): yp,
        (0, -1, 0): ym,
        (0, 0, 1): base + bz,
        (0, 0, -1): base - bz,
        (1, 1, 0): xp + by,
        (-1, 1, 0): xm + by,
        (1, -1, 0): xp - by,
        (-1, -1, 0): xm - by,
        (1, 0, 1): xp + bz,
        (-1, 0, 1): xm + bz,
        (1, 0, -1): xp - bz,
        (-1, 0, -1): xm - bz,
        (0, 1, 1): yp + bz,
        (0, -1, 1): ym + bz,
        (0, 1, -1): yp - bz,
        (0, -1, -1): ym - bz,
    }
    for q in range(19):
        emit(q, along[STENCIL[q]] + (1.0 - OMEGA) * g[q])


def output(
    stored_in,
    adj_in,
    low,
    high,
    left,
    right,
    grad,
    out_hbm,
    grad_hbm,
    stored,
    adj,
    out,
    in_sems,
    out_sems,
):
    low_on, high_on, left_on, right_on = ends()
    reads, writes = [], []
    for n in range(GROUPS):
        part = pl.ds(n * STEP, STEP)
        for k, (src, dst) in enumerate(((adj_in, adj), (stored_in, stored))):
            copy = pltpu.make_async_copy(src.at[:, part], dst.at[:, part], in_sems.at[k, n])
            copy.start()
            reads.append(copy)
    copy = pltpu.make_async_copy(grad, grad_hbm, out_sems.at[GROUPS])
    copy.start()
    writes.append(copy)

    def plane(x, taken=(), ref=None, on=None):
        f = [stored[q, x].astype(jnp.float32) for q in range(19)]
        g = []
        for q in range(19):
            at = x + STENCIL[q][0]
            if q in taken:
                n = taken.index(q)
                g.append(ref[n * Z : (n + 1) * Z, :] * on)
            else:
                g.append(pulled_z(adj, q, at, low, high, at, low_on, high_on))

        def emit(q, value):
            out[q, x] = value

        collide_transpose(f, g, emit)

    def body(x, carry):
        plane(x)
        return carry

    done = 0
    for n in range(GROUPS):
        reads[2 * n].wait()
        reads[2 * n + 1].wait()
        ready = (n + 1) * STEP - 1
        if n == 0:
            plane(0, X_DOWN, left, left_on)
        lax.fori_loop(max(done, 1), ready, body, 0)
        if n == GROUPS - 1:
            plane(X - 1, X_UP, right, right_on)
            ready = X
        part = pl.ds(done, ready - done)
        copy = pltpu.make_async_copy(out.at[:, part], out_hbm.at[:, part], out_sems.at[n])
        copy.start()
        writes.append(copy)
        done = ready
    for copy in writes:
        copy.wait()


def put(split, at, tile):
    head = tile.astype(jnp.bfloat16)
    split[pl.ds(at, tile.shape[0]), :] = head
    rest = (tile - head.astype(jnp.float32)).astype(jnp.bfloat16)
    split[pl.ds(split.shape[0] // 2 + at, tile.shape[0]), :] = rest


def bases(cell, where):
    cells = cell[:, where]
    bx = jnp.broadcast_to(cells >> 11, (8, CHUNK))
    bz = jnp.broadcast_to((cells >> 8) & 7, (8, CHUNK))
    return bx, bz


def pick(dx, three):
    return jnp.where(
        dx == -1, three[0], jnp.where(dx == 0, three[1], jnp.where(dx == 1, three[2], 0.0))
    )


def gathered(split, rows, hot, factors):
    picked = jnp.dot(split[...], hot, preferred_element_type=jnp.float32)
    half = split.shape[0] // 2
    out = []
    for d in range(3):
        summed = None
        for t, factor in enumerate(factors):
            at = d * rows + 8 * t
            term = factor * (picked[at : at + 8] + picked[half + at : half + at + 8])
            summed = term if summed is None else summed + term
        out.append(summed)
    return out


def sublanes():
    return lax.broadcasted_iota(jnp.int32, (8, CHUNK), 0)


def chunk_of(c):
    return pl.ds(pl.multiple_of(c * CHUNK, CHUNK), CHUNK)


def weights_of(weight, where):
    return [jnp.broadcast_to(weight[s : s + 1, where], (8, CHUNK)) for s in range(9)]


def stage_a(count, adj, rho, cell, weight, live_weight, hot, acc, near, split):
    rows = X * Z
    for k, x in enumerate(NEAR):
        near[:, k] = adj[:, x]
    for x in range(0, X, 2):
        scale = 3.0 * rho[x * Z : (x + 2) * Z, :]
        first, second = column(adj, x), column(adj, x + 1)
        for d in range(3):
            put(split, d * rows + x * Z, scale * jnp.concatenate([first[d], second[d]]))
    lanes = lax.broadcasted_iota(jnp.int32, (9, CHUNK), 1)

    def chunk(c, carry):
        where = chunk_of(c)
        live = (lanes + c * CHUNK) < count[0]
        live_weight[:, where] = jnp.where(live, weight[:, where], 0.0)
        w = weights_of(live_weight, where)
        y_of = jnp.broadcast_to(cell[:, where] & (Y - 1), (Y, CHUNK))
        one = jnp.where(lax.broadcasted_iota(jnp.int32, (Y, CHUNK), 0) == y_of, 1.0, 0.0)
        one = one.astype(jnp.bfloat16)
        hot[:, where] = one
        bx, bz = bases(cell, where)
        dz = sublanes() - bz
        three = [pick(dz, w[3 * a : 3 * a + 3]) for a in range(3)]
        factors = [pick(x - bx, three) for x in range(X)]
        for d, tile in enumerate(gathered(split, rows, one, factors)):
            acc[d, :, where] = tile
        return carry

    lax.fori_loop(0, cell.shape[1] // CHUNK, chunk, 0, unroll=4)


def stage_b(
    sent_low, sent_high, low, high, cell, panel, weight, hot, acc_in, acc, which, split
):
    low_on, high_on, _, _ = ends()
    rows = 4 * X
    for k, (sent, up, back, ref, on) in enumerate(
        (
            (sent_low, Z_UP, Z_DOWN, low, low_on),
            (sent_high, Z_DOWN, Z_UP, high, high_on),
        )
    ):
        beyond, _, _ = edge_moments(sent, up)
        added, _, _ = edge_moments(ref, back)
        here = 3.0 * sent[Z_RHO : Z_RHO + X, :] * on
        there = 3.0 * ref[Z_RHO : Z_RHO + X, :]
        for d in range(3):
            put(split, d * rows + k * X, here * added[d])
            mom = beyond[d] + ref[Z_MOM + d * X : Z_MOM + (d + 1) * X, :]
            put(split, d * rows + (2 + k) * X, there * mom)

    def chunk(c, carry):
        where = chunk_of(c)
        w = weights_of(weight, where)
        bx, bz = bases(cell, where)
        sub = sublanes()
        dx = [sub - bx, sub + 8 - bx]
        first, last, under, over = [], [], [], []
        for a in range(3):
            wa = w[3 * a : 3 * a + 3]
            first.append(jnp.where(bz == 0, wa[1], jnp.where(bz == 1, wa[0], 0.0)))
            last.append(jnp.where(bz == Z - 1, wa[1], jnp.where(bz == Z - 2, wa[2], 0.0)))
            under.append(jnp.where(bz == 0, wa[0], 0.0))
            over.append(jnp.where(bz == Z - 1, wa[2], 0.0))
        factors = [pick(at, three) for three in (first, last, under, over) for at in dx]
        for d, tile in enumerate(gathered(split, rows, hot[:, where], factors)):
            acc[d, :, where] = acc_in[d, :, where] + tile
        panels = jnp.broadcast_to(panel[:, where], (PANELS, CHUNK))
        match = lax.broadcasted_iota(jnp.int32, (PANELS, CHUNK), 0) == panels
        which[:, where] = jnp.where(match, 1.0, 0.0).astype(jnp.bfloat16)
        return carry

    lax.fori_loop(0, cell.shape[1] // CHUNK, chunk, 0, unroll=4)


def stage_c(
    rho,
    sent_left,
    sent_right,
    low,
    high,
    along,
    across,
    cell,
    weight,
    hot,
    which,
    acc_in,
    grad,
    partial,
    left,
    right,
    split,
    totals,
):
    low_on, high_on, left_on, right_on = ends()
    by_parity(lax.axis_index(GX), right, left, across, along)
    rows = 48
    zero = jnp.zeros((8, Y), jnp.float32)
    beyond, added = [], []
    for sent, ref, on, pops, back, x in (
        (sent_left, left, left_on, X_UP, X_DOWN, 0),
        (sent_right, right, right_on, X_DOWN, X_UP, X - 1),
    ):
        g, h = [None] * 19, [None] * 19
        for n in range(5):
            g[pops[n]] = sent[n * Z : (n + 1) * Z, :]
            h[back[n]] = ref[n * Z : (n + 1) * Z, :]
        there = 3.0 * ref[X_RHO : X_RHO + Z, :]
        here = 3.0 * on * rho[x * Z : (x + 1) * Z, :]
        beyond.append(
            [
                there * (ref[X_MOM + d * Z : X_MOM + (d + 1) * Z, :] + mom)
                for d, mom in enumerate(first_moments(g))
            ]
        )
        added.append([here * mom for mom in first_moments(h)])
    for d in range(3):
        corner = []
        for k, (ref, on) in enumerate(((low, low_on), (high, high_on))):
            at, far = X_EDGE + 3 * k + d, X_FAR + 3 * k + d
            for mine, theirs in ((sent_left, left), (sent_right, right)):
                scale = 3.0 * theirs[X_EDGE + 6 + k : X_EDGE + 7 + k, :]
                corner.append(scale * (theirs[at : at + 1, :] + mine[far : far + 1, :]))
            for theirs, x, side_on in ((left, 0, left_on), (right, X - 1, right_on)):
                scale = 3.0 * on * side_on * row(ref, Z_RHO + x)
                corner.append(scale * theirs[far : far + 1, :])
        tiles = [beyond[0][d], beyond[1][d], added[0][d], added[1][d], jnp.concatenate(corner), zero]
        for t in range(0, 6, 2):
            put(split, d * rows + t * 8, jnp.concatenate(tiles[t : t + 2]))

    sub = sublanes()
    kind = sub & 3
    corner_x = jnp.where(kind == 0, -1, jnp.where(kind == 1, X, jnp.where(kind == 2, 0, X - 1)))
    bottom = sub < 4

    def chunk(c, carry):
        where = chunk_of(c)
        w = weights_of(weight, where)
        bx, bz = bases(cell, where)
        dz = sub - bz
        at_low, at_high = bottom & (bz == 0), (sub >= 4) & (bz == Z - 1)
        inner, corner = [], []
        for a in range(3):
            wa = w[3 * a : 3 * a + 3]
            inner.append(pick(dz, wa))
            corner.append(jnp.where(at_low, wa[0], jnp.where(at_high, wa[2], 0.0)))
        factors = [
            jnp.where(bx == 0, inner[0], 0.0),
            jnp.where(bx == X - 1, inner[2], 0.0),
            jnp.where(bx == 0, inner[1], jnp.where(bx == 1, inner[0], 0.0)),
            jnp.where(bx == X - 1, inner[1], jnp.where(bx == X - 2, inner[2], 0.0)),
            pick(corner_x - bx, corner),
        ]
        sums = []
        for d, tile in enumerate(gathered(split, rows, hot[:, where], factors)):
            sums.append(jnp.sum(acc_in[d, :, where] + tile, axis=0, keepdims=True))
            grad[d : d + 1, where] = sums[d]
        sums = jnp.concatenate(sums + [jnp.zeros((5, CHUNK), jnp.float32)])
        top = sums.astype(jnp.bfloat16)
        rest = (sums - top.astype(jnp.float32)).astype(jnp.bfloat16)
        totals[:, where] = jnp.concatenate([top, rest])
        return carry

    lax.fori_loop(0, cell.shape[1] // CHUNK, chunk, 0, unroll=UNROLL_C)
    total = lax.dot_general(
        totals[...], which[...], (((1,), (1,)), ((), ())), preferred_element_type=jnp.float32
    )
    result = total[0:3] + total[8:11]
    result = jnp.concatenate([result[0:1], result[1:2], result[2:3]], axis=1)
    for n in range(partial.shape[0]):
        partial[n] = result


def exchange_z(across, along):
    count = lax.axis_size(GZ)
    along = lax.ppermute(
        along, GZ, [(i, (i + 1 if i % 2 else i - 1) % count) for i in range(count)]
    )
    return lax.ppermute(across, GZ, [(i, i ^ 1) for i in range(count)]), along


def exchange_x(across, along):
    count, width = lax.axis_size(GX), lax.axis_size(GZ)
    pairs = []
    for i in range(count):
        for j in range(width):
            if i in (0, count - 1):
                to = i * width + (j ^ 1)
            else:
                to = (i + 1 if i % 2 else i - 1) * width + j
            pairs.append((i * width + j, to))
    along = lax.ppermute(along, GX + GZ, pairs)
    return lax.ppermute(across, GX, [(i, i ^ 1) for i in range(count)]), along


PARAMS = pltpu.CompilerParams(vmem_limit_bytes=48 * 1024 * 1024)
FIRST_BIG = pltpu.CompilerParams(vmem_limit_bytes=53 * 1024 * 1024)
BIG = pltpu.CompilerParams(vmem_limit_bytes=52 * 1024 * 1024)


def cost(flops, moved):
    return pl.CostEstimate(flops=flops, bytes_accessed=moved, transcendentals=0)


def shape(*dims):
    return jax.ShapeDtypeStruct(dims, jnp.float32)


def summed(parts, count):
    total = jnp.sum(parts, axis=0)
    return jnp.broadcast_to(total[None], (count,) + total.shape)


def local(stored, adj, marker_cell, marker_weight, marker_panel, marker_count):
    slots = marker_cell.shape[0]
    whole = pl.BlockSpec(memory_space=pltpu.VMEM)
    hbm = pl.BlockSpec(memory_space=pltpu.HBM)
    any_space = pl.BlockSpec(memory_space=pl.ANY)
    cell, panel = marker_cell.reshape(1, slots), marker_panel.reshape(1, slots)
    to_low, to_high, across, along, rho = pl.pallas_call(
        pack_z,
        out_shape=(
            shape(ZROWS, Y),
            shape(ZROWS, Y),
            shape(ZROWS, Y),
            shape(ZROWS, Y),
            shape(X * Z, Y),
        ),
        in_specs=[hbm, hbm],
        out_specs=(whole,) * 5,
        scratch_shapes=[
            pltpu.VMEM(stored.shape, stored.dtype),
            pltpu.VMEM(adj.shape, adj.dtype),
            pltpu.SemaphoreType.DMA((3, GROUPS)),
        ],
        compiler_params=FIRST_BIG,
        cost_estimate=cost(5_000_000, 4_000_000),
    )(stored, adj)
    across, along = exchange_z(across, along)
    weight, hot, acc, near = pl.pallas_call(
        stage_a,
        out_shape=(
            shape(9, slots),
            jax.ShapeDtypeStruct((Y, slots), jnp.bfloat16),
            shape(3, 8, slots),
            shape(19, len(NEAR), Z, Y),
        ),
        in_specs=[pl.BlockSpec(memory_space=pltpu.SMEM)] + [whole] * 4,
        scratch_shapes=[pltpu.VMEM((6 * X * Z, Y), jnp.bfloat16)],
        compiler_params=PARAMS,
        cost_estimate=cost(800_000_000, 2_000_000),
    )(marker_count, adj, rho, cell, marker_weight)
    to_left, to_right, across, along, low, high = pl.pallas_call(
        pack_x,
        out_shape=(shape(XROWS, Y),) * 4 + (shape(ZROWS, Y),) * 2,
        in_specs=[whole] * 6 + [any_space],
        compiler_params=PARAMS,
        cost_estimate=cost(1_000_000, 2_000_000),
    )(near, rho, to_low, to_high, along, across, acc)
    across, along = exchange_x(across, along)
    acc, which = pl.pallas_call(
        stage_b,
        out_shape=(shape(3, 8, slots), jax.ShapeDtypeStruct((PANELS, slots), jnp.bfloat16)),
        scratch_shapes=[pltpu.VMEM((24 * X, Y), jnp.bfloat16)],
        compiler_params=PARAMS,
        cost_estimate=cost(400_000_000, 2_000_000),
    )(to_low, to_high, low, high, cell, panel, weight, hot, acc)
    grad, partial, left, right = pl.pallas_call(
        stage_c,
        out_shape=(
            shape(3, slots),
            shape(lax.axis_size(FIRST), 1, 3 * PANELS),
            shape(XROWS, Y),
            shape(XROWS, Y),
        ),
        scratch_shapes=[
            pltpu.VMEM((6 * 48, Y), jnp.bfloat16),
            pltpu.VMEM((16, slots), jnp.bfloat16),
        ],
        compiler_params=PARAMS,
        cost_estimate=cost(300_000_000, 2_000_000),
    )(rho, to_left, to_right, low, high, along, across, cell, weight, hot, which, acc)
    out, grad = pl.pallas_call(
        output,
        out_shape=(shape(19, X, Z, Y), shape(3, slots)),
        in_specs=[hbm, hbm] + [whole] * 5,
        out_specs=(hbm, hbm),
        scratch_shapes=[
            pltpu.VMEM(stored.shape, stored.dtype),
            pltpu.VMEM(adj.shape, adj.dtype),
            pltpu.VMEM(adj.shape, adj.dtype),
            pltpu.SemaphoreType.DMA((2, GROUPS)),
            pltpu.SemaphoreType.DMA((GROUPS + 1,)),
        ],
        compiler_params=BIG,
        cost_estimate=cost(10_000_000, 7_000_000),
    )(stored, adj, low, high, left, right, grad)
    partial = summed(lax.all_to_all(partial, FIRST, 0, 0), lax.axis_size(SECOND))
    total = jnp.sum(lax.all_to_all(partial, SECOND, 0, 0), axis=0).reshape(3, PANELS)
    return (out, grad, total)


def solution(mesh):
    split = jax.sharding.Mesh(
        mesh.devices.reshape(4, 4, 4, 2, 2), ("y", "zh", "x", "zl", "core")
    )
    return jax.shard_map(
        local,
        mesh=split,
        in_specs=(
            P(None, GX, GZ, None),
            P(None, GX, GZ, None),
            P(GX + GZ),
            P(None, GX + GZ),
            P(GX + GZ),
            P(GX + GZ),
        ),
        out_specs=(P(None, GX, GZ, None), P(None, GX + GZ), P()),
        check_vma=False,
    )
```

```python
import functools

import jax
import jax.numpy as jnp
from jax import lax
from jax.experimental import pallas as pl
from jax.experimental.pallas import tpu as pltpu
from jax.sharding import PartitionSpec as P

PANELS = 128
STENCIL = [
    (0, 0, 0),
    (1, 0, 0),
    (-1, 0, 0),
    (0, 1, 0),
    (0, -1, 0),
    (0, 0, 1),
    (0, 0, -1),
    (1, 1, 0),
    (-1, 1, 0),
    (1, -1, 0),
    (-1, -1, 0),
    (1, 0, 1),
    (-1, 0, 1),
    (1, 0, -1),
    (-1, 0, -1),
    (0, 1, 1),
    (0, -1, 1),
    (0, 1, -1),
    (0, -1, -1),
]
W0, W1, W2 = 1.0 / 3.0, 1.0 / 18.0, 1.0 / 36.0
WEIGHTS = [W0] + [W1] * 6 + [W2] * 12
OMEGA = 1.6

X, Z, Y = 16, 8, 256
X_UP = [q for q in range(19) if STENCIL[q][0] == 1]
X_DOWN = [q for q in range(19) if STENCIL[q][0] == -1]
Z_UP = [q for q in range(19) if STENCIL[q][2] == 1]
Z_DOWN = [q for q in range(19) if STENCIL[q][2] == -1]

ZROWS, Z_RHO, Z_MOM, Z_SPILL = 152, 80, 96, 144
XROWS, X_MOM, X_RHO, X_EDGE, X_FAR = 88, 40, 64, 72, 80

GX = ("y", "zh")
GZ = ("x", "zl", "core")
FIRST = ("core", "zh", "zl")
SECOND = ("y", "x")

CHUNK = 256
UNROLL_C = 8
GROUPS = 4
STEP = X // GROUPS
NEAR = (0, 1, X - 2, X - 1)


def roll_y(tile, q):
    step = STENCIL[q][1]
    if step == 0:
        return tile
    return pltpu.roll(tile, (-step) % Y, tile.ndim - 1)


def first_moments(g):
    def total(terms):
        out = None
        for q, sign in terms:
            if g[q] is None:
                continue
            if out is None:
                out = g[q] if sign > 0 else -g[q]
            else:
                out = out + g[q] if sign > 0 else out - g[q]
        return out

    parts = []
    for d in range(3):
        axis = total([(q, STENCIL[q][d]) for q in range(1, 7) if STENCIL[q][d]])
        diag = total([(q, STENCIL[q][d]) for q in range(7, 19) if STENCIL[q][d]])
        if axis is None and diag is None:
            parts.append(None)
        elif axis is None:
            parts.append(W2 * diag)
        elif diag is None:
            parts.append(W1 * axis)
        else:
            parts.append(W1 * axis + W2 * diag)
    return parts


def z_shift(tile, q, low, high):
    step = STENCIL[q][2]
    if step == 0:
        return tile
    rows = lax.broadcasted_iota(jnp.int32, tile.shape, 0)
    halo, edge = (high, Z - 1) if step > 0 else (low, 0)
    if halo is None:
        halo = jnp.zeros_like(tile)
    return jnp.where(rows == edge, halo, pltpu.roll(tile, (-step) % Z, 0))


def pulled_own(adj, q, x):
    return roll_y(z_shift(adj[q, x], q, None, None), q)


def row(ref, index):
    return ref[pl.ds(index, 1), :]


def pulled_z(adj, q, x, low, high, plane, low_on, high_on):
    step = STENCIL[q][2]
    lo = hi = None
    if step < 0:
        lo = row(low, Z_DOWN.index(q) * X + x) * low_on
    if step > 0:
        hi = row(high, Z_UP.index(q) * X + x) * high_on
    return roll_y(z_shift(adj[q, plane], q, lo, hi), q)


def ends():
    gz, gx = lax.axis_index(GZ), lax.axis_index(GX)
    gz_n, gx_n = lax.axis_size(GZ), lax.axis_size(GX)
    flag = lambda c: jnp.where(c, 1.0, 0.0).astype(jnp.float32)
    return flag(gz > 0), flag(gz < gz_n - 1), flag(gx > 0), flag(gx < gx_n - 1)


def column(adj, x):
    g = [None] * 19
    for q in range(1, 19):
        at = x + STENCIL[q][0]
        if 0 <= at < X:
            g[q] = pulled_own(adj, q, at)
    return first_moments(g)


def by_parity(index, first, second, even_first, even_second):
    even = lax.rem(index, 2) == 0
    a, b = even_first[...], even_second[...]
    first[...] = jnp.where(even, a, b)
    second[...] = jnp.where(even, b, a)


def pack_z(stored_in, adj_in, to_low, to_high, across, along, rho_out, stored, adj, sems):
    copies = []
    for n in range(GROUPS):
        part = pl.ds(n * STEP, STEP)
        group = []
        for k, first in enumerate((0, Z - 2)):
            at = (pl.ds(1, 18), part, pl.ds(first, 2))
            group.append(pltpu.make_async_copy(adj_in.at[at], adj.at[at], sems.at[k, n]))
        group.append(
            pltpu.make_async_copy(stored_in.at[:, part], stored.at[:, part], sems.at[2, n])
        )
        for copy in group:
            copy.start()
        copies.append(group)

    def density(x):
        rho = stored[0, x].astype(jnp.float32)
        for q in range(1, 19):
            rho = rho + stored[q, x].astype(jnp.float32)
        rho_out[pl.ds(x * Z, Z), :] = rho
        to_low[pl.ds(Z_RHO + x, 1), :] = rho[0:1]
        to_high[pl.ds(Z_RHO + x, 1), :] = rho[Z - 1 : Z]
        for n in range(5):
            to_low[pl.ds(n * X + x, 1), :] = adj[Z_UP[n], x, 0:1, :]
            to_high[pl.ds(n * X + x, 1), :] = adj[Z_DOWN[n], x, Z - 1 : Z, :]

    def moments(x):
        for d, mom in enumerate(column(adj, x)):
            to_low[pl.ds(Z_MOM + d * X + x, 1), :] = mom[0:1]
            to_high[pl.ds(Z_MOM + d * X + x, 1), :] = mom[Z - 1 : Z]

    for n in range(GROUPS):
        for copy in copies[n]:
            copy.wait()
        first, last = n * STEP, (n + 1) * STEP
        for x in range(first, last):
            density(x)
        for x in range(max(first - 1, 0), last if n == GROUPS - 1 else last - 1):
            moments(x)
    spill = [column(adj, -1), column(adj, X)]
    zero = jnp.zeros((1, Y), jnp.float32)
    low_rows, high_rows = [], []
    for d in range(3):
        for side in range(2):
            mom = spill[side][d]
            low_rows.append(zero if mom is None else mom[0:1])
            high_rows.append(zero if mom is None else mom[Z - 1 : Z])
    to_low[Z_SPILL:, :] = jnp.concatenate(low_rows + [zero, zero])
    to_high[Z_SPILL:, :] = jnp.concatenate(high_rows + [zero, zero])
    by_parity(lax.axis_index(GZ), across, along, to_high, to_low)


def shift_rows(tile, step):
    if step == 0:
        return tile
    rows = lax.broadcasted_iota(jnp.int32, tile.shape, 0)
    edge = X - 1 if step > 0 else 0
    return jnp.where(rows == edge, 0.0, pltpu.roll(tile, (-step) % X, 0))


def edge_moments(sent, pops):
    tiles, before, after = [None] * 19, [None] * 19, [None] * 19
    for n, q in enumerate(pops):
        tile = roll_y(sent[n * X : (n + 1) * X, :], q)
        step = STENCIL[q][0]
        tiles[q] = shift_rows(tile, step)
        if step > 0:
            before[q] = tile[0:1]
        if step < 0:
            after[q] = tile[X - 1 : X]
    return first_moments(tiles), first_moments(before), first_moments(after)


def plus(a, b):
    return a if b is None else a + b


def pack_x(
    near,
    rho,
    sent_low,
    sent_high,
    along_in,
    across_in,
    after,
    to_left,
    to_right,
    across,
    along,
    low,
    high,
):
    del after
    by_parity(lax.axis_index(GZ), high, low, across_in, along_in)
    low_on, high_on, _, _ = ends()
    edge_low, edge_high = edge_moments(sent_low, Z_UP), edge_moments(sent_high, Z_DOWN)

    def side(out, x, plane, inner, away, skip):
        for n, q in enumerate(away):
            out[n * Z : (n + 1) * Z, :] = pulled_z(
                near, q, x, low, high, plane, low_on, high_on
            )
        g = [None] * 19
        for q in range(1, 19):
            step = STENCIL[q][0]
            if step == 0:
                g[q] = pulled_z(near, q, x, low, high, plane, low_on, high_on)
            elif step != skip:
                g[q] = pulled_z(near, q, x + step, low, high, inner, low_on, high_on)
        for d, mom in enumerate(first_moments(g)):
            out[X_MOM + d * Z : X_MOM + (d + 1) * Z, :] = mom
        out[X_RHO : X_RHO + Z, :] = rho[x * Z : (x + 1) * Z, :]
        beyond = 1 if x > 0 else 0
        edge, far = [], []
        for ref, own, on in ((low, edge_low, low_on), (high, edge_high, high_on)):
            for d in range(3):
                here = row(ref, Z_MOM + d * X + x) * on
                edge.append(here + own[0][d][x : x + 1])
                there = row(ref, Z_SPILL + 2 * d + beyond) * on
                far.append(plus(there, own[1 + beyond][d]))
        for ref, on in ((low, low_on), (high, high_on)):
            edge.append(row(ref, Z_RHO + x) * on)
        out[X_EDGE : X_EDGE + 8, :] = jnp.concatenate(edge)
        far = far + [jnp.zeros((1, Y), jnp.float32)] * 2
        out[X_FAR : X_FAR + 8, :] = jnp.concatenate(far)

    side(to_left, 0, 0, 1, X_UP, -1)
    side(to_right, X - 1, 3, 2, X_DOWN, 1)
    by_parity(lax.axis_index(GX), across, along, to_right, to_left)


def collide_transpose(f, g, emit):
    rho = f[0]
    for q in range(1, 19):
        rho = rho + f[q]
    jx = (f[1] - f[2]) + (f[7] - f[8]) + (f[9] - f[10]) + (f[11] - f[12]) + (f[13] - f[14])
    jy = (f[3] - f[4]) + (f[7] - f[9]) + (f[8] - f[10]) + (f[15] - f[16]) + (f[17] - f[18])
    jz = (f[5] - f[6]) + (f[11] - f[13]) + (f[12] - f[14]) + (f[15] - f[17]) + (f[16] - f[18])
    inv = 1.0 / rho
    ux, uy, uz = jx * inv, jy * inv, jz * inv

    sx, sy, sz = W1 * (g[1] + g[2]), W1 * (g[3] + g[4]), W1 * (g[5] + g[6])
    dx, dy, dz = W1 * (g[1] - g[2]), W1 * (g[3] - g[4]), W1 * (g[5] - g[6])

    def plane(a, b, c, d):
        p, m = g[a] + g[d], g[b] + g[c]
        r, s = g[a] - g[d], g[b] - g[c]
        return W2 * (p + m), W2 * (p - m), W2 * (r - s), W2 * (r + s)

    s_xy, c_xy, xy_x, xy_y = plane(7, 8, 9, 10)
    s_xz, c_xz, xz_x, xz_z = plane(11, 12, 13, 14)
    s_yz, c_yz, yz_y, yz_z = plane(15, 16, 17, 18)
    m_x = dx + xy_x + xz_x
    m_y = dy + xy_y + yz_y
    m_z = dz + xz_z + yz_z
    g_xx = sx + s_xy + s_xz
    g_yy = sy + s_xy + s_yz
    g_zz = sz + s_xz + s_yz
    g0 = W0 * g[0] + (sx + sy + sz) + (s_xy + s_xz + s_yz)
    vx = g_xx * ux + c_xy * uy + c_xz * uz
    vy = c_xy * ux + g_yy * uy + c_yz * uz
    vz = c_xz * ux + c_yz * uy + g_zz * uz
    uv = ux * vx + uy * vy + uz * vz
    uu = ux * ux + uy * uy + uz * uz
    base = OMEGA * (g0 - 4.5 * uv + 1.5 * uu * g0)
    bx = OMEGA * (3.0 * m_x + 9.0 * vx - 3.0 * ux * g0)
    by = OMEGA * (3.0 * m_y + 9.0 * vy - 3.0 * uy * g0)
    bz = OMEGA * (3.0 * m_z + 9.0 * vz - 3.0 * uz * g0)
    xp, xm = base + bx, base - bx
    yp, ym = base + by, base - by
    along = {
        (0, 0, 0): base,
        (1, 0, 0): xp,
        (-1, 0, 0): xm,
        (0, 1, 0): yp,
        (0, -1, 0): ym,
        (0, 0, 1): base + bz,
        (0, 0, -1): base - bz,
        (1, 1, 0): xp + by,
        (-1, 1, 0): xm + by,
        (1, -1, 0): xp - by,
        (-1, -1, 0): xm - by,
        (1, 0, 1): xp + bz,
        (-1, 0, 1): xm + bz,
        (1, 0, -1): xp - bz,
        (-1, 0, -1): xm - bz,
        (0, 1, 1): yp + bz,
        (0, -1, 1): ym + bz,
        (0, 1, -1): yp - bz,
        (0, -1, -1): ym - bz,
    }
    for q in range(19):
        emit(q, along[STENCIL[q]] + (1.0 - OMEGA) * g[q])


def interior(stored, adj, low, high, after, out_hbm, token, ends_stored, out, sems):
    del after
    low_on, high_on, _, _ = ends()

    def body(x, carry):
        f = [stored[q, x].astype(jnp.float32) for q in range(19)]
        g = []
        for q in range(19):
            at = x + STENCIL[q][0]
            g.append(pulled_z(adj, q, at, low, high, at, low_on, high_on))

        def emit(q, value):
            out[q, x] = value

        collide_transpose(f, g, emit)
        return carry

    writes = []
    for n, (first, last) in enumerate(((1, 5), (5, 9), (9, 13), (13, X - 1))):
        lax.fori_loop(first, last, body, 0)
        part = pl.ds(first, last - first)
        copy = pltpu.make_async_copy(out.at[:, part], out_hbm.at[:, part], sems.at[n])
        copy.start()
        writes.append(copy)
    for k, x in enumerate((0, X - 1)):
        ends_stored[k] = stored[:, x].astype(jnp.float32)
    token[...] = jnp.zeros_like(token)
    for copy in writes:
        copy.wait()


def finish(
    parts,
    grad,
    near,
    ends_stored,
    low,
    high,
    left,
    right,
    out_in,
    out,
    grad_hbm,
    panel_hbm,
    planes,
    panel,
    sems,
):
    del out_in
    low_on, high_on, left_on, right_on = ends()
    total = parts[0]
    for n in range(1, parts.shape[0]):
        total = total + parts[n]
    for d in range(3):
        panel[d : d + 1, :] = total[:, d * PANELS : (d + 1) * PANELS]
    writes = [
        pltpu.make_async_copy(panel, panel_hbm, sems.at[0]),
        pltpu.make_async_copy(grad, grad_hbm, sems.at[1]),
    ]
    for copy in writes:
        copy.start()
    for k, (x, plane, inner, taken, ref, on) in enumerate(
        (
            (0, 0, 1, X_DOWN, left, left_on),
            (X - 1, 3, 2, X_UP, right, right_on),
        )
    ):
        f = [ends_stored[k, q] for q in range(19)]
        g = []
        for q in range(19):
            step = STENCIL[q][0]
            if q in taken:
                n = taken.index(q)
                g.append(ref[n * Z : (n + 1) * Z, :] * on)
            else:
                at = plane if step == 0 else inner
                g.append(pulled_z(near, q, x + step, low, high, at, low_on, high_on))

        def emit(q, value, k=k):
            planes[k, q] = value

        collide_transpose(f, g, emit)
        copy = pltpu.make_async_copy(planes.at[k], out.at[:, x], sems.at[2 + k])
        copy.start()
        writes.append(copy)
    for copy in writes:
        copy.wait()


def put(split, at, tile):
    head = tile.astype(jnp.bfloat16)
    split[pl.ds(at, tile.shape[0]), :] = head
    rest = (tile - head.astype(jnp.float32)).astype(jnp.bfloat16)
    split[pl.ds(split.shape[0] // 2 + at, tile.shape[0]), :] = rest


def bases(cell, where):
    cells = cell[:, where]
    bx = jnp.broadcast_to(cells >> 11, (8, CHUNK))
    bz = jnp.broadcast_to((cells >> 8) & 7, (8, CHUNK))
    return bx, bz


def pick(dx, three):
    return jnp.where(
        dx == -1, three[0], jnp.where(dx == 0, three[1], jnp.where(dx == 1, three[2], 0.0))
    )


def gathered(split, rows, hot, factors):
    picked = jnp.dot(split[...], hot, preferred_element_type=jnp.float32)
    half = split.shape[0] // 2
    out = []
    for d in range(3):
        summed = None
        for t, factor in enumerate(factors):
            at = d * rows + 8 * t
            term = factor * (picked[at : at + 8] + picked[half + at : half + at + 8])
            summed = term if summed is None else summed + term
        out.append(summed)
    return out


def sublanes():
    return lax.broadcasted_iota(jnp.int32, (8, CHUNK), 0)


def chunk_of(c):
    return pl.ds(pl.multiple_of(c * CHUNK, CHUNK), CHUNK)


def weights_of(weight, where):
    return [jnp.broadcast_to(weight[s : s + 1, where], (8, CHUNK)) for s in range(9)]


def stage_a(count, adj, rho, cell, weight, live_weight, hot, acc, near, split):
    rows = X * Z
    for k, x in enumerate(NEAR):
        near[:, k] = adj[:, x]
    for x in range(0, X, 2):
        scale = 3.0 * rho[x * Z : (x + 2) * Z, :]
        first, second = column(adj, x), column(adj, x + 1)
        for d in range(3):
            put(split, d * rows + x * Z, scale * jnp.concatenate([first[d], second[d]]))
    lanes = lax.broadcasted_iota(jnp.int32, (9, CHUNK), 1)

    def chunk(c, carry):
        where = chunk_of(c)
        live = (lanes + c * CHUNK) < count[0]
        live_weight[:, where] = jnp.where(live, weight[:, where], 0.0)
        w = weights_of(live_weight, where)
        y_of = jnp.broadcast_to(cell[:, where] & (Y - 1), (Y, CHUNK))
        one = jnp.where(lax.broadcasted_iota(jnp.int32, (Y, CHUNK), 0) == y_of, 1.0, 0.0)
        one = one.astype(jnp.bfloat16)
        hot[:, where] = one
        bx, bz = bases(cell, where)
        dz = sublanes() - bz
        three = [pick(dz, w[3 * a : 3 * a + 3]) for a in range(3)]
        factors = [pick(x - bx, three) for x in range(X)]
        for d, tile in enumerate(gathered(split, rows, one, factors)):
            acc[d, :, where] = tile
        return carry

    lax.fori_loop(0, cell.shape[1] // CHUNK, chunk, 0, unroll=4)


def stage_b(
    sent_low, sent_high, low, high, cell, panel, weight, hot, acc_in, acc, which, split
):
    low_on, high_on, _, _ = ends()
    rows = 4 * X
    for k, (sent, up, back, ref, on) in enumerate(
        (
            (sent_low, Z_UP, Z_DOWN, low, low_on),
            (sent_high, Z_DOWN, Z_UP, high, high_on),
        )
    ):
        beyond, _, _ = edge_moments(sent, up)
        added, _, _ = edge_moments(ref, back)
        here = 3.0 * sent[Z_RHO : Z_RHO + X, :] * on
        there = 3.0 * ref[Z_RHO : Z_RHO + X, :]
        for d in range(3):
            put(split, d * rows + k * X, here * added[d])
            mom = beyond[d] + ref[Z_MOM + d * X : Z_MOM + (d + 1) * X, :]
            put(split, d * rows + (2 + k) * X, there * mom)

    def chunk(c, carry):
        where = chunk_of(c)
        w = weights_of(weight, where)
        bx, bz = bases(cell, where)
        sub = sublanes()
        dx = [sub - bx, sub + 8 - bx]
        first, last, under, over = [], [], [], []
        for a in range(3):
            wa = w[3 * a : 3 * a + 3]
            first.append(jnp.where(bz == 0, wa[1], jnp.where(bz == 1, wa[0], 0.0)))
            last.append(jnp.where(bz == Z - 1, wa[1], jnp.where(bz == Z - 2, wa[2], 0.0)))
            under.append(jnp.where(bz == 0, wa[0], 0.0))
            over.append(jnp.where(bz == Z - 1, wa[2], 0.0))
        factors = [pick(at, three) for three in (first, last, under, over) for at in dx]
        for d, tile in enumerate(gathered(split, rows, hot[:, where], factors)):
            acc[d, :, where] = acc_in[d, :, where] + tile
        panels = jnp.broadcast_to(panel[:, where], (PANELS, CHUNK))
        match = lax.broadcasted_iota(jnp.int32, (PANELS, CHUNK), 0) == panels
        which[:, where] = jnp.where(match, 1.0, 0.0).astype(jnp.bfloat16)
        return carry

    lax.fori_loop(0, cell.shape[1] // CHUNK, chunk, 0, unroll=4)


def stage_c(
    rho,
    sent_left,
    sent_right,
    low,
    high,
    along,
    across,
    cell,
    weight,
    hot,
    which,
    acc_in,
    token,
    grad,
    partial,
    left,
    right,
    split,
    totals,
):
    del token
    low_on, high_on, left_on, right_on = ends()
    by_parity(lax.axis_index(GX), right, left, across, along)
    rows = 48
    zero = jnp.zeros((8, Y), jnp.float32)
    beyond, added = [], []
    for sent, ref, on, pops, back, x in (
        (sent_left, left, left_on, X_UP, X_DOWN, 0),
        (sent_right, right, right_on, X_DOWN, X_UP, X - 1),
    ):
        g, h = [None] * 19, [None] * 19
        for n in range(5):
            g[pops[n]] = sent[n * Z : (n + 1) * Z, :]
            h[back[n]] = ref[n * Z : (n + 1) * Z, :]
        there = 3.0 * ref[X_RHO : X_RHO + Z, :]
        here = 3.0 * on * rho[x * Z : (x + 1) * Z, :]
        beyond.append(
            [
                there * (ref[X_MOM + d * Z : X_MOM + (d + 1) * Z, :] + mom)
                for d, mom in enumerate(first_moments(g))
            ]
        )
        added.append([here * mom for mom in first_moments(h)])
    for d in range(3):
        corner = []
        for k, (ref, on) in enumerate(((low, low_on), (high, high_on))):
            at, far = X_EDGE + 3 * k + d, X_FAR + 3 * k + d
            for mine, theirs in ((sent_left, left), (sent_right, right)):
                scale = 3.0 * theirs[X_EDGE + 6 + k : X_EDGE + 7 + k, :]
                corner.append(scale * (theirs[at : at + 1, :] + mine[far : far + 1, :]))
            for theirs, x, side_on in ((left, 0, left_on), (right, X - 1, right_on)):
                scale = 3.0 * on * side_on * row(ref, Z_RHO + x)
                corner.append(scale * theirs[far : far + 1, :])
        tiles = [beyond[0][d], beyond[1][d], added[0][d], added[1][d], jnp.concatenate(corner), zero]
        for t in range(0, 6, 2):
            put(split, d * rows + t * 8, jnp.concatenate(tiles[t : t + 2]))

    sub = sublanes()
    kind = sub & 3
    corner_x = jnp.where(kind == 0, -1, jnp.where(kind == 1, X, jnp.where(kind == 2, 0, X - 1)))
    bottom = sub < 4

    def chunk(c, carry):
        where = chunk_of(c)
        w = weights_of(weight, where)
        bx, bz = bases(cell, where)
        dz = sub - bz
        at_low, at_high = bottom & (bz == 0), (sub >= 4) & (bz == Z - 1)
        inner, corner = [], []
        for a in range(3):
            wa = w[3 * a : 3 * a + 3]
            inner.append(pick(dz, wa))
            corner.append(jnp.where(at_low, wa[0], jnp.where(at_high, wa[2], 0.0)))
        factors = [
            jnp.where(bx == 0, inner[0], 0.0),
            jnp.where(bx == X - 1, inner[2], 0.0),
            jnp.where(bx == 0, inner[1], jnp.where(bx == 1, inner[0], 0.0)),
            jnp.where(bx == X - 1, inner[1], jnp.where(bx == X - 2, inner[2], 0.0)),
            pick(corner_x - bx, corner),
        ]
        sums = []
        for d, tile in enumerate(gathered(split, rows, hot[:, where], factors)):
            sums.append(jnp.sum(acc_in[d, :, where] + tile, axis=0, keepdims=True))
            grad[d : d + 1, where] = sums[d]
        sums = jnp.concatenate(sums + [jnp.zeros((5, CHUNK), jnp.float32)])
        top = sums.astype(jnp.bfloat16)
        rest = (sums - top.astype(jnp.float32)).astype(jnp.bfloat16)
        totals[:, where] = jnp.concatenate([top, rest])
        return carry

    lax.fori_loop(0, cell.shape[1] // CHUNK, chunk, 0, unroll=UNROLL_C)
    total = lax.dot_general(
        totals[...], which[...], (((1,), (1,)), ((), ())), preferred_element_type=jnp.float32
    )
    result = total[0:3] + total[8:11]
    result = jnp.concatenate([result[0:1], result[1:2], result[2:3]], axis=1)
    for n in range(partial.shape[0]):
        partial[n] = result


def exchange_z(across, along):
    count = lax.axis_size(GZ)
    along = lax.ppermute(
        along, GZ, [(i, (i + 1 if i % 2 else i - 1) % count) for i in range(count)]
    )
    return lax.ppermute(across, GZ, [(i, i ^ 1) for i in range(count)]), along


def exchange_x(across, along):
    count, width = lax.axis_size(GX), lax.axis_size(GZ)
    pairs = []
    for i in range(count):
        for j in range(width):
            if i in (0, count - 1):
                to = i * width + (j ^ 1)
            else:
                to = (i + 1 if i % 2 else i - 1) * width + j
            pairs.append((i * width + j, to))
    along = lax.ppermute(along, GX + GZ, pairs)
    return lax.ppermute(across, GX, [(i, i ^ 1) for i in range(count)]), along


PARAMS = pltpu.CompilerParams(vmem_limit_bytes=48 * 1024 * 1024)
FIRST_BIG = pltpu.CompilerParams(vmem_limit_bytes=53 * 1024 * 1024)
BIG = pltpu.CompilerParams(vmem_limit_bytes=52 * 1024 * 1024)


def cost(flops, moved):
    return pl.CostEstimate(flops=flops, bytes_accessed=moved, transcendentals=0)


def shape(*dims):
    return jax.ShapeDtypeStruct(dims, jnp.float32)


def summed(parts, count):
    total = jnp.sum(parts, axis=0)
    return jnp.broadcast_to(total[None], (count,) + total.shape)


def local(stored, adj, marker_cell, marker_weight, marker_panel, marker_count):
    slots = marker_cell.shape[0]
    whole = pl.BlockSpec(memory_space=pltpu.VMEM)
    hbm = pl.BlockSpec(memory_space=pltpu.HBM)
    any_space = pl.BlockSpec(memory_space=pl.ANY)
    cell, panel = marker_cell.reshape(1, slots), marker_panel.reshape(1, slots)
    to_low, to_high, across, along, rho = pl.pallas_call(
        pack_z,
        out_shape=(
            shape(ZROWS, Y),
            shape(ZROWS, Y),
            shape(ZROWS, Y),
            shape(ZROWS, Y),
            shape(X * Z, Y),
        ),
        in_specs=[hbm, hbm],
        out_specs=(whole,) * 5,
        scratch_shapes=[
            pltpu.VMEM(stored.shape, stored.dtype),
            pltpu.VMEM(adj.shape, adj.dtype),
            pltpu.SemaphoreType.DMA((3, GROUPS)),
        ],
        compiler_params=FIRST_BIG,
        cost_estimate=cost(5_000_000, 4_000_000),
    )(stored, adj)
    across, along = exchange_z(across, along)
    weight, hot, acc, near = pl.pallas_call(
        stage_a,
        out_shape=(
            shape(9, slots),
            jax.ShapeDtypeStruct((Y, slots), jnp.bfloat16),
            shape(3, 8, slots),
            shape(19, len(NEAR), Z, Y),
        ),
        in_specs=[pl.BlockSpec(memory_space=pltpu.SMEM)] + [whole] * 4,
        scratch_shapes=[pltpu.VMEM((6 * X * Z, Y), jnp.bfloat16)],
        compiler_params=PARAMS,
        cost_estimate=cost(800_000_000, 2_000_000),
    )(marker_count, adj, rho, cell, marker_weight)
    to_left, to_right, across, along, low, high = pl.pallas_call(
        pack_x,
        out_shape=(shape(XROWS, Y),) * 4 + (shape(ZROWS, Y),) * 2,
        in_specs=[whole] * 6 + [any_space],
        compiler_params=PARAMS,
        cost_estimate=cost(1_000_000, 2_000_000),
    )(near, rho, to_low, to_high, along, across, acc)
    across, along = exchange_x(across, along)
    acc, which = pl.pallas_call(
        stage_b,
        out_shape=(shape(3, 8, slots), jax.ShapeDtypeStruct((PANELS, slots), jnp.bfloat16)),
        scratch_shapes=[pltpu.VMEM((24 * X, Y), jnp.bfloat16)],
        compiler_params=PARAMS,
        cost_estimate=cost(400_000_000, 2_000_000),
    )(to_low, to_high, low, high, cell, panel, weight, hot, acc)
    out, token, ends_stored = pl.pallas_call(
        interior,
        out_shape=(shape(19, X, Z, Y), shape(8, PANELS), shape(2, 19, Z, Y)),
        out_specs=(hbm, whole, whole),
        scratch_shapes=[
            pltpu.VMEM(adj.shape, adj.dtype),
            pltpu.SemaphoreType.DMA((GROUPS,)),
        ],
        compiler_params=PARAMS,
        cost_estimate=cost(10_000_000, 7_000_000),
    )(stored, adj, low, high, acc)
    grad, partial, left, right = pl.pallas_call(
        stage_c,
        out_shape=(
            shape(3, slots),
            shape(lax.axis_size(FIRST), 1, 3 * PANELS),
            shape(XROWS, Y),
            shape(XROWS, Y),
        ),
        scratch_shapes=[
            pltpu.VMEM((6 * 48, Y), jnp.bfloat16),
            pltpu.VMEM((16, slots), jnp.bfloat16),
        ],
        compiler_params=PARAMS,
        cost_estimate=cost(300_000_000, 2_000_000),
    )(rho, to_left, to_right, low, high, along, across, cell, weight, hot, which, acc, token)
    partial = summed(lax.all_to_all(partial, FIRST, 0, 0), lax.axis_size(SECOND))
    partial = lax.all_to_all(partial, SECOND, 0, 0)
    return pl.pallas_call(
        finish,
        out_shape=(shape(19, X, Z, Y), shape(3, slots), shape(3, PANELS)),
        in_specs=[whole] * 8 + [any_space],
        out_specs=(any_space, hbm, hbm),
        scratch_shapes=[
            pltpu.VMEM((2, 19, Z, Y), jnp.float32),
            pltpu.VMEM((3, PANELS), jnp.float32),
            pltpu.SemaphoreType.DMA((4,)),
        ],
        input_output_aliases={8: 0},
        compiler_params=PARAMS,
        cost_estimate=cost(1_000_000, 2_000_000),
    )(partial, grad, near, ends_stored, low, high, left, right, out)


def solution(mesh):
    split = jax.sharding.Mesh(
        mesh.devices.reshape(4, 4, 4, 2, 2), ("y", "zh", "x", "zl", "core")
    )
    return jax.shard_map(
        local,
        mesh=split,
        in_specs=(
            P(None, GX, GZ, None),
            P(None, GX, GZ, None),
            P(GX + GZ),
            P(None, GX + GZ),
            P(GX + GZ),
            P(GX + GZ),
        ),
        out_specs=(P(None, GX, GZ, None), P(None, GX + GZ), P()),
        check_vma=False,
    )
```

```python
import functools

import jax
import jax.numpy as jnp
from jax import lax
from jax.experimental import pallas as pl
from jax.experimental.pallas import tpu as pltpu
from jax.sharding import PartitionSpec as P

PANELS = 128
STENCIL = [
    (0, 0, 0),
    (1, 0, 0),
    (-1, 0, 0),
    (0, 1, 0),
    (0, -1, 0),
    (0, 0, 1),
    (0, 0, -1),
    (1, 1, 0),
    (-1, 1, 0),
    (1, -1, 0),
    (-1, -1, 0),
    (1, 0, 1),
    (-1, 0, 1),
    (1, 0, -1),
    (-1, 0, -1),
    (0, 1, 1),
    (0, -1, 1),
    (0, 1, -1),
    (0, -1, -1),
]
W0, W1, W2 = 1.0 / 3.0, 1.0 / 18.0, 1.0 / 36.0
WEIGHTS = [W0] + [W1] * 6 + [W2] * 12
OMEGA = 1.6

X, Z, Y = 16, 8, 256
X_UP = [q for q in range(19) if STENCIL[q][0] == 1]
X_DOWN = [q for q in range(19) if STENCIL[q][0] == -1]
Z_UP = [q for q in range(19) if STENCIL[q][2] == 1]
Z_DOWN = [q for q in range(19) if STENCIL[q][2] == -1]

ZROWS, Z_RHO, Z_MOM, Z_SPILL = 152, 80, 96, 144
XROWS, X_MOM, X_RHO, X_EDGE, X_FAR = 88, 40, 64, 72, 80

GX = ("y", "zh")
GZ = ("x", "zl", "core")
FIRST = ("core", "zh", "zl")
SECOND = ("y", "x")

CHUNK = 256
UNROLL_C = 8
GROUPS = 4
PARTS = 2
STEP = X // GROUPS
NEAR = (0, 1, X - 2, X - 1)


def roll_y(tile, q):
    step = STENCIL[q][1]
    if step == 0:
        return tile
    return pltpu.roll(tile, (-step) % Y, tile.ndim - 1)


def first_moments(g):
    def total(terms):
        out = None
        for q, sign in terms:
            if g[q] is None:
                continue
            if out is None:
                out = g[q] if sign > 0 else -g[q]
            else:
                out = out + g[q] if sign > 0 else out - g[q]
        return out

    parts = []
    for d in range(3):
        axis = total([(q, STENCIL[q][d]) for q in range(1, 7) if STENCIL[q][d]])
        diag = total([(q, STENCIL[q][d]) for q in range(7, 19) if STENCIL[q][d]])
        if axis is None and diag is None:
            parts.append(None)
        elif axis is None:
            parts.append(W2 * diag)
        elif diag is None:
            parts.append(W1 * axis)
        else:
            parts.append(W1 * axis + W2 * diag)
    return parts


def z_shift(tile, q, low, high):
    step = STENCIL[q][2]
    if step == 0:
        return tile
    rows = lax.broadcasted_iota(jnp.int32, tile.shape, 0)
    halo, edge = (high, Z - 1) if step > 0 else (low, 0)
    if halo is None:
        halo = jnp.zeros_like(tile)
    return jnp.where(rows == edge, halo, pltpu.roll(tile, (-step) % Z, 0))


def pulled_own(adj, q, x):
    return roll_y(z_shift(adj[q, x], q, None, None), q)


def row(ref, index):
    return ref[pl.ds(index, 1), :]


def pulled_z(adj, q, x, low, high, plane, low_on, high_on):
    step = STENCIL[q][2]
    lo = hi = None
    if step < 0:
        lo = row(low, Z_DOWN.index(q) * X + x) * low_on
    if step > 0:
        hi = row(high, Z_UP.index(q) * X + x) * high_on
    return roll_y(z_shift(adj[q, plane], q, lo, hi), q)


def ends():
    gz, gx = lax.axis_index(GZ), lax.axis_index(GX)
    gz_n, gx_n = lax.axis_size(GZ), lax.axis_size(GX)
    flag = lambda c: jnp.where(c, 1.0, 0.0).astype(jnp.float32)
    return flag(gz > 0), flag(gz < gz_n - 1), flag(gx > 0), flag(gx < gx_n - 1)


def column(adj, x):
    g = [None] * 19
    for q in range(1, 19):
        at = x + STENCIL[q][0]
        if 0 <= at < X:
            g[q] = pulled_own(adj, q, at)
    return first_moments(g)


def by_parity(index, first, second, even_first, even_second):
    even = lax.rem(index, 2) == 0
    a, b = even_first[...], even_second[...]
    first[...] = jnp.where(even, a, b)
    second[...] = jnp.where(even, b, a)


def pack_z(stored_in, adj_in, to_low, to_high, across, along, rho_out, stored, adj, sems):
    copies = []
    for n in range(PARTS):
        part = pl.ds(n * (X // PARTS), (X // PARTS))
        group = []
        for k, first in enumerate((0, Z - 2)):
            at = (pl.ds(1, 18), part, pl.ds(first, 2))
            group.append(pltpu.make_async_copy(adj_in.at[at], adj.at[at], sems.at[k, n]))
        group.append(
            pltpu.make_async_copy(stored_in.at[:, part], stored.at[:, part], sems.at[2, n])
        )
        for copy in group:
            copy.start()
        copies.append(group)

    def density(x):
        rho = stored[0, x].astype(jnp.float32)
        for q in range(1, 19):
            rho = rho + stored[q, x].astype(jnp.float32)
        rho_out[pl.ds(x * Z, Z), :] = rho
        to_low[pl.ds(Z_RHO + x, 1), :] = rho[0:1]
        to_high[pl.ds(Z_RHO + x, 1), :] = rho[Z - 1 : Z]
        for n in range(5):
            to_low[pl.ds(n * X + x, 1), :] = adj[Z_UP[n], x, 0:1, :]
            to_high[pl.ds(n * X + x, 1), :] = adj[Z_DOWN[n], x, Z - 1 : Z, :]

    def moments(x):
        for d, mom in enumerate(column(adj, x)):
            to_low[pl.ds(Z_MOM + d * X + x, 1), :] = mom[0:1]
            to_high[pl.ds(Z_MOM + d * X + x, 1), :] = mom[Z - 1 : Z]

    for n in range(PARTS):
        for copy in copies[n]:
            copy.wait()
        first, last = n * (X // PARTS), (n + 1) * (X // PARTS)
        for x in range(first, last):
            density(x)
        for x in range(max(first - 1, 0), last if n == PARTS - 1 else last - 1):
            moments(x)
    spill = [column(adj, -1), column(adj, X)]
    zero = jnp.zeros((1, Y), jnp.float32)
    low_rows, high_rows = [], []
    for d in range(3):
        for side in range(2):
            mom = spill[side][d]
            low_rows.append(zero if mom is None else mom[0:1])
            high_rows.append(zero if mom is None else mom[Z - 1 : Z])
    to_low[Z_SPILL:, :] = jnp.concatenate(low_rows + [zero, zero])
    to_high[Z_SPILL:, :] = jnp.concatenate(high_rows + [zero, zero])
    by_parity(lax.axis_index(GZ), across, along, to_high, to_low)


def shift_rows(tile, step):
    if step == 0:
        return tile
    rows = lax.broadcasted_iota(jnp.int32, tile.shape, 0)
    edge = X - 1 if step > 0 else 0
    return jnp.where(rows == edge, 0.0, pltpu.roll(tile, (-step) % X, 0))


def edge_moments(sent, pops):
    tiles, before, after = [None] * 19, [None] * 19, [None] * 19
    for n, q in enumerate(pops):
        tile = roll_y(sent[n * X : (n + 1) * X, :], q)
        step = STENCIL[q][0]
        tiles[q] = shift_rows(tile, step)
        if step > 0:
            before[q] = tile[0:1]
        if step < 0:
            after[q] = tile[X - 1 : X]
    return first_moments(tiles), first_moments(before), first_moments(after)


def plus(a, b):
    return a if b is None else a + b


def pack_x(
    near,
    rho,
    sent_low,
    sent_high,
    along_in,
    across_in,
    after,
    to_left,
    to_right,
    across,
    along,
    low,
    high,
):
    del after
    by_parity(lax.axis_index(GZ), high, low, across_in, along_in)
    low_on, high_on, _, _ = ends()
    edge_low, edge_high = edge_moments(sent_low, Z_UP), edge_moments(sent_high, Z_DOWN)

    def side(out, x, plane, inner, away, skip):
        for n, q in enumerate(away):
            out[n * Z : (n + 1) * Z, :] = pulled_z(
                near, q, x, low, high, plane, low_on, high_on
            )
        g = [None] * 19
        for q in range(1, 19):
            step = STENCIL[q][0]
            if step == 0:
                g[q] = pulled_z(near, q, x, low, high, plane, low_on, high_on)
            elif step != skip:
                g[q] = pulled_z(near, q, x + step, low, high, inner, low_on, high_on)
        for d, mom in enumerate(first_moments(g)):
            out[X_MOM + d * Z : X_MOM + (d + 1) * Z, :] = mom
        out[X_RHO : X_RHO + Z, :] = rho[x * Z : (x + 1) * Z, :]
        beyond = 1 if x > 0 else 0
        edge, far = [], []
        for ref, own, on in ((low, edge_low, low_on), (high, edge_high, high_on)):
            for d in range(3):
                here = row(ref, Z_MOM + d * X + x) * on
                edge.append(here + own[0][d][x : x + 1])
                there = row(ref, Z_SPILL + 2 * d + beyond) * on
                far.append(plus(there, own[1 + beyond][d]))
        for ref, on in ((low, low_on), (high, high_on)):
            edge.append(row(ref, Z_RHO + x) * on)
        out[X_EDGE : X_EDGE + 8, :] = jnp.concatenate(edge)
        far = far + [jnp.zeros((1, Y), jnp.float32)] * 2
        out[X_FAR : X_FAR + 8, :] = jnp.concatenate(far)

    side(to_left, 0, 0, 1, X_UP, -1)
    side(to_right, X - 1, 3, 2, X_DOWN, 1)
    by_parity(lax.axis_index(GX), across, along, to_right, to_left)


def collide_transpose(f, g, emit):
    rho = f[0]
    for q in range(1, 19):
        rho = rho + f[q]
    jx = (f[1] - f[2]) + (f[7] - f[8]) + (f[9] - f[10]) + (f[11] - f[12]) + (f[13] - f[14])
    jy = (f[3] - f[4]) + (f[7] - f[9]) + (f[8] - f[10]) + (f[15] - f[16]) + (f[17] - f[18])
    jz = (f[5] - f[6]) + (f[11] - f[13]) + (f[12] - f[14]) + (f[15] - f[17]) + (f[16] - f[18])
    inv = 1.0 / rho
    ux, uy, uz = jx * inv, jy * inv, jz * inv

    sx, sy, sz = W1 * (g[1] + g[2]), W1 * (g[3] + g[4]), W1 * (g[5] + g[6])
    dx, dy, dz = W1 * (g[1] - g[2]), W1 * (g[3] - g[4]), W1 * (g[5] - g[6])

    def plane(a, b, c, d):
        p, m = g[a] + g[d], g[b] + g[c]
        r, s = g[a] - g[d], g[b] - g[c]
        return W2 * (p + m), W2 * (p - m), W2 * (r - s), W2 * (r + s)

    s_xy, c_xy, xy_x, xy_y = plane(7, 8, 9, 10)
    s_xz, c_xz, xz_x, xz_z = plane(11, 12, 13, 14)
    s_yz, c_yz, yz_y, yz_z = plane(15, 16, 17, 18)
    m_x = dx + xy_x + xz_x
    m_y = dy + xy_y + yz_y
    m_z = dz + xz_z + yz_z
    g_xx = sx + s_xy + s_xz
    g_yy = sy + s_xy + s_yz
    g_zz = sz + s_xz + s_yz
    g0 = W0 * g[0] + (sx + sy + sz) + (s_xy + s_xz + s_yz)
    vx = g_xx * ux + c_xy * uy + c_xz * uz
    vy = c_xy * ux + g_yy * uy + c_yz * uz
    vz = c_xz * ux + c_yz * uy + g_zz * uz
    uv = ux * vx + uy * vy + uz * vz
    uu = ux * ux + uy * uy + uz * uz
    base = OMEGA * (g0 - 4.5 * uv + 1.5 * uu * g0)
    bx = OMEGA * (3.0 * m_x + 9.0 * vx - 3.0 * ux * g0)
    by = OMEGA * (3.0 * m_y + 9.0 * vy - 3.0 * uy * g0)
    bz = OMEGA * (3.0 * m_z + 9.0 * vz - 3.0 * uz * g0)
    xp, xm = base + bx, base - bx
    yp, ym = base + by, base - by
    along = {
        (0, 0, 0): base,
        (1, 0, 0): xp,
        (-1, 0, 0): xm,
        (0, 1, 0): yp,
        (0, -1, 0): ym,
        (0, 0, 1): base + bz,
        (0, 0, -1): base - bz,
        (1, 1, 0): xp + by,
        (-1, 1, 0): xm + by,
        (1, -1, 0): xp - by,
        (-1, -1, 0): xm - by,
        (1, 0, 1): xp + bz,
        (-1, 0, 1): xm + bz,
        (1, 0, -1): xp - bz,
        (-1, 0, -1): xm - bz,
        (0, 1, 1): yp + bz,
        (0, -1, 1): ym + bz,
        (0, 1, -1): yp - bz,
        (0, -1, -1): ym - bz,
    }
    for q in range(19):
        emit(q, along[STENCIL[q]] + (1.0 - OMEGA) * g[q])


def interior(stored, adj, low, high, after, out_hbm, token, ends_stored, out, sems):
    del after
    low_on, high_on, _, _ = ends()

    def body(x, carry):
        f = [stored[q, x].astype(jnp.float32) for q in range(19)]
        g = []
        for q in range(19):
            at = x + STENCIL[q][0]
            g.append(pulled_z(adj, q, at, low, high, at, low_on, high_on))

        def emit(q, value):
            out[q, x] = value

        collide_transpose(f, g, emit)
        return carry

    writes = []
    for n, (first, last) in enumerate(((1, 5), (5, 9), (9, 13), (13, X - 1))):
        lax.fori_loop(first, last, body, 0)
        part = pl.ds(first, last - first)
        copy = pltpu.make_async_copy(out.at[:, part], out_hbm.at[:, part], sems.at[n])
        copy.start()
        writes.append(copy)
    for k, x in enumerate((0, X - 1)):
        ends_stored[k] = stored[:, x].astype(jnp.float32)
    token[...] = jnp.zeros_like(token)
    for copy in writes:
        copy.wait()


def finish(
    parts,
    grad,
    near,
    ends_stored,
    low,
    high,
    left,
    right,
    out_in,
    out,
    grad_hbm,
    panel_hbm,
    planes,
    panel,
    sems,
):
    del out_in
    low_on, high_on, left_on, right_on = ends()
    total = parts[0]
    for n in range(1, parts.shape[0]):
        total = total + parts[n]
    for d in range(3):
        panel[d : d + 1, :] = total[:, d * PANELS : (d + 1) * PANELS]
    writes = [
        pltpu.make_async_copy(panel, panel_hbm, sems.at[0]),
        pltpu.make_async_copy(grad, grad_hbm, sems.at[1]),
    ]
    for copy in writes:
        copy.start()
    for k, (x, plane, inner, taken, ref, on) in enumerate(
        (
            (0, 0, 1, X_DOWN, left, left_on),
            (X - 1, 3, 2, X_UP, right, right_on),
        )
    ):
        f = [ends_stored[k, q] for q in range(19)]
        g = []
        for q in range(19):
            step = STENCIL[q][0]
            if q in taken:
                n = taken.index(q)
                g.append(ref[n * Z : (n + 1) * Z, :] * on)
            else:
                at = plane if step == 0 else inner
                g.append(pulled_z(near, q, x + step, low, high, at, low_on, high_on))

        def emit(q, value, k=k):
            planes[k, q] = value

        collide_transpose(f, g, emit)
        copy = pltpu.make_async_copy(planes.at[k], out.at[:, x], sems.at[2 + k])
        copy.start()
        writes.append(copy)
    for copy in writes:
        copy.wait()


def put(split, at, tile):
    head = tile.astype(jnp.bfloat16)
    split[pl.ds(at, tile.shape[0]), :] = head
    rest = (tile - head.astype(jnp.float32)).astype(jnp.bfloat16)
    split[pl.ds(split.shape[0] // 2 + at, tile.shape[0]), :] = rest


def bases(cell, where):
    cells = cell[:, where]
    bx = jnp.broadcast_to(cells >> 11, (8, CHUNK))
    bz = jnp.broadcast_to((cells >> 8) & 7, (8, CHUNK))
    return bx, bz


def pick(dx, three):
    return jnp.where(
        dx == -1, three[0], jnp.where(dx == 0, three[1], jnp.where(dx == 1, three[2], 0.0))
    )


def gathered(split, rows, hot, factors):
    picked = jnp.dot(split[...], hot, preferred_element_type=jnp.float32)
    half = split.shape[0] // 2
    out = []
    for d in range(3):
        summed = None
        for t, factor in enumerate(factors):
            at = d * rows + 8 * t
            term = factor * (picked[at : at + 8] + picked[half + at : half + at + 8])
            summed = term if summed is None else summed + term
        out.append(summed)
    return out


def sublanes():
    return lax.broadcasted_iota(jnp.int32, (8, CHUNK), 0)


def chunk_of(c):
    return pl.ds(pl.multiple_of(c * CHUNK, CHUNK), CHUNK)


def weights_of(weight, where):
    return [jnp.broadcast_to(weight[s : s + 1, where], (8, CHUNK)) for s in range(9)]


def stage_a(count, adj_in, rho, cell, weight, live_weight, hot, acc, near, adj, split, sems):
    rows = X * Z
    copies = []
    for n in range(GROUPS):
        part = pl.ds(n * STEP, STEP)
        copy = pltpu.make_async_copy(adj_in.at[:, part], adj.at[:, part], sems.at[n])
        copy.start()
        copies.append(copy)
    lanes = lax.broadcasted_iota(jnp.int32, (9, CHUNK), 1)

    def prepare(c, carry):
        where = chunk_of(c)
        live = (lanes + c * CHUNK) < count[0]
        live_weight[:, where] = jnp.where(live, weight[:, where], 0.0)
        y_of = jnp.broadcast_to(cell[:, where] & (Y - 1), (Y, CHUNK))
        one = jnp.where(lax.broadcasted_iota(jnp.int32, (Y, CHUNK), 0) == y_of, 1.0, 0.0)
        hot[:, where] = one.astype(jnp.bfloat16)
        return carry

    lax.fori_loop(0, cell.shape[1] // CHUNK, prepare, 0, unroll=2)
    done = 0
    for n in range(GROUPS):
        copies[n].wait()
        ready = X if n == GROUPS - 1 else (n + 1) * STEP - 2
        for x in range(done, ready, 2):
            scale = 3.0 * rho[x * Z : (x + 2) * Z, :]
            first, second = column(adj, x), column(adj, x + 1)
            for d in range(3):
                put(split, d * rows + x * Z, scale * jnp.concatenate([first[d], second[d]]))
        done = ready
    for k, x in enumerate(NEAR):
        near[:, k] = adj[:, x]

    def chunk(c, carry):
        where = chunk_of(c)
        w = weights_of(live_weight, where)
        bx, bz = bases(cell, where)
        dz = sublanes() - bz
        three = [pick(dz, w[3 * a : 3 * a + 3]) for a in range(3)]
        factors = [pick(x - bx, three) for x in range(X)]
        for d, tile in enumerate(gathered(split, rows, hot[:, where], factors)):
            acc[d, :, where] = tile
        return carry

    lax.fori_loop(0, cell.shape[1] // CHUNK, chunk, 0, unroll=4)


def shares(sub, bx, bz, w):
    kind = sub & 3
    corner_x = jnp.where(kind == 0, -1, jnp.where(kind == 1, X, jnp.where(kind == 2, 0, X - 1)))
    dz = sub - bz
    at_low, at_high = (sub < 4) & (bz == 0), (sub >= 4) & (bz == Z - 1)
    inner, corner = [], []
    for a in range(3):
        wa = w[3 * a : 3 * a + 3]
        inner.append(pick(dz, wa))
        corner.append(jnp.where(at_low, wa[0], jnp.where(at_high, wa[2], 0.0)))
    return [
        jnp.where(bx == 0, inner[0], 0.0),
        jnp.where(bx == X - 1, inner[2], 0.0),
        jnp.where(bx == 0, inner[1], jnp.where(bx == 1, inner[0], 0.0)),
        jnp.where(bx == X - 1, inner[1], jnp.where(bx == X - 2, inner[2], 0.0)),
        pick(corner_x - bx, corner),
    ]


def stage_b(
    sent_low, sent_high, low, high, cell, panel, weight, hot, acc_in, acc, which, share, split
):
    low_on, high_on, _, _ = ends()
    rows = 4 * X
    for k, (sent, up, back, ref, on) in enumerate(
        (
            (sent_low, Z_UP, Z_DOWN, low, low_on),
            (sent_high, Z_DOWN, Z_UP, high, high_on),
        )
    ):
        beyond, _, _ = edge_moments(sent, up)
        added, _, _ = edge_moments(ref, back)
        here = 3.0 * sent[Z_RHO : Z_RHO + X, :] * on
        there = 3.0 * ref[Z_RHO : Z_RHO + X, :]
        for d in range(3):
            put(split, d * rows + k * X, here * added[d])
            mom = beyond[d] + ref[Z_MOM + d * X : Z_MOM + (d + 1) * X, :]
            put(split, d * rows + (2 + k) * X, there * mom)

    def chunk(c, carry):
        where = chunk_of(c)
        w = weights_of(weight, where)
        bx, bz = bases(cell, where)
        sub = sublanes()
        for t, tile in enumerate(shares(sub, bx, bz, w)):
            share[8 * t : 8 * t + 8, where] = tile
        dx = [sub - bx, sub + 8 - bx]
        first, last, under, over = [], [], [], []
        for a in range(3):
            wa = w[3 * a : 3 * a + 3]
            first.append(jnp.where(bz == 0, wa[1], jnp.where(bz == 1, wa[0], 0.0)))
            last.append(jnp.where(bz == Z - 1, wa[1], jnp.where(bz == Z - 2, wa[2], 0.0)))
            under.append(jnp.where(bz == 0, wa[0], 0.0))
            over.append(jnp.where(bz == Z - 1, wa[2], 0.0))
        factors = [pick(at, three) for three in (first, last, under, over) for at in dx]
        for d, tile in enumerate(gathered(split, rows, hot[:, where], factors)):
            acc[d, :, where] = acc_in[d, :, where] + tile
        panels = jnp.broadcast_to(panel[:, where], (PANELS, CHUNK))
        match = lax.broadcasted_iota(jnp.int32, (PANELS, CHUNK), 0) == panels
        rows_at = pl.ds(pl.multiple_of(c * CHUNK, CHUNK), CHUNK)
        which[rows_at, :] = jnp.where(match, 1.0, 0.0).T.astype(jnp.bfloat16)
        return carry

    lax.fori_loop(0, cell.shape[1] // CHUNK, chunk, 0, unroll=4)


def stage_c(
    rho,
    sent_left,
    sent_right,
    low,
    high,
    along,
    across,
    share,
    hot,
    which,
    acc_in,
    token,
    grad,
    partial,
    left,
    right,
    split,
    totals,
):
    del token
    low_on, high_on, left_on, right_on = ends()
    by_parity(lax.axis_index(GX), right, left, across, along)
    rows = 48
    zero = jnp.zeros((8, Y), jnp.float32)
    beyond, added = [], []
    for sent, ref, on, pops, back, x in (
        (sent_left, left, left_on, X_UP, X_DOWN, 0),
        (sent_right, right, right_on, X_DOWN, X_UP, X - 1),
    ):
        g, h = [None] * 19, [None] * 19
        for n in range(5):
            g[pops[n]] = sent[n * Z : (n + 1) * Z, :]
            h[back[n]] = ref[n * Z : (n + 1) * Z, :]
        there = 3.0 * ref[X_RHO : X_RHO + Z, :]
        here = 3.0 * on * rho[x * Z : (x + 1) * Z, :]
        beyond.append(
            [
                there * (ref[X_MOM + d * Z : X_MOM + (d + 1) * Z, :] + mom)
                for d, mom in enumerate(first_moments(g))
            ]
        )
        added.append([here * mom for mom in first_moments(h)])
    for d in range(3):
        corner = []
        for k, (ref, on) in enumerate(((low, low_on), (high, high_on))):
            at, far = X_EDGE + 3 * k + d, X_FAR + 3 * k + d
            for mine, theirs in ((sent_left, left), (sent_right, right)):
                scale = 3.0 * theirs[X_EDGE + 6 + k : X_EDGE + 7 + k, :]
                corner.append(scale * (theirs[at : at + 1, :] + mine[far : far + 1, :]))
            for theirs, x, side_on in ((left, 0, left_on), (right, X - 1, right_on)):
                scale = 3.0 * on * side_on * row(ref, Z_RHO + x)
                corner.append(scale * theirs[far : far + 1, :])
        tiles = [beyond[0][d], beyond[1][d], added[0][d], added[1][d], jnp.concatenate(corner), zero]
        for t in range(0, 6, 2):
            put(split, d * rows + t * 8, jnp.concatenate(tiles[t : t + 2]))

    def chunk(c, carry):
        where = chunk_of(c)
        factors = [share[8 * t : 8 * t + 8, where] for t in range(5)]
        sums = []
        for d, tile in enumerate(gathered(split, rows, hot[:, where], factors)):
            sums.append(jnp.sum(acc_in[d, :, where] + tile, axis=0, keepdims=True))
            grad[d : d + 1, where] = sums[d]
        sums = jnp.concatenate(sums + [jnp.zeros((5, CHUNK), jnp.float32)])
        top = sums.astype(jnp.bfloat16)
        rest = (sums - top.astype(jnp.float32)).astype(jnp.bfloat16)
        totals[:, where] = jnp.concatenate([top, rest])
        return carry

    lax.fori_loop(0, hot.shape[1] // CHUNK, chunk, 0, unroll=UNROLL_C)
    total = jnp.dot(totals[...], which[...], preferred_element_type=jnp.float32)
    result = total[0:3] + total[8:11]
    result = jnp.concatenate([result[0:1], result[1:2], result[2:3]], axis=1)
    for n in range(partial.shape[0]):
        partial[n] = result


def exchange_z(across, along):
    count = lax.axis_size(GZ)
    along = lax.ppermute(
        along, GZ, [(i, (i + 1 if i % 2 else i - 1) % count) for i in range(count)]
    )
    return lax.ppermute(across, GZ, [(i, i ^ 1) for i in range(count)]), along


def exchange_x(across, along):
    count, width = lax.axis_size(GX), lax.axis_size(GZ)
    pairs = []
    for i in range(count):
        for j in range(width):
            if i in (0, count - 1):
                to = i * width + (j ^ 1)
            else:
                to = (i + 1 if i % 2 else i - 1) * width + j
            pairs.append((i * width + j, to))
    along = lax.ppermute(along, GX + GZ, pairs)
    return lax.ppermute(across, GX, [(i, i ^ 1) for i in range(count)]), along


PARAMS = pltpu.CompilerParams(vmem_limit_bytes=48 * 1024 * 1024)
MID = pltpu.CompilerParams(vmem_limit_bytes=50 * 1024 * 1024)
FIRST_BIG = pltpu.CompilerParams(vmem_limit_bytes=53 * 1024 * 1024)
BIG = pltpu.CompilerParams(vmem_limit_bytes=52 * 1024 * 1024)


def cost(flops, moved):
    return pl.CostEstimate(flops=flops, bytes_accessed=moved, transcendentals=0)


def shape(*dims):
    return jax.ShapeDtypeStruct(dims, jnp.float32)


def summed(parts, count):
    total = jnp.sum(parts, axis=0)
    return jnp.broadcast_to(total[None], (count,) + total.shape)


def local(stored, adj, marker_cell, marker_weight, marker_panel, marker_count):
    slots = marker_cell.shape[0]
    whole = pl.BlockSpec(memory_space=pltpu.VMEM)
    hbm = pl.BlockSpec(memory_space=pltpu.HBM)
    any_space = pl.BlockSpec(memory_space=pl.ANY)
    cell, panel = marker_cell.reshape(1, slots), marker_panel.reshape(1, slots)
    to_low, to_high, across, along, rho = pl.pallas_call(
        pack_z,
        out_shape=(
            shape(ZROWS, Y),
            shape(ZROWS, Y),
            shape(ZROWS, Y),
            shape(ZROWS, Y),
            shape(X * Z, Y),
        ),
        in_specs=[hbm, hbm],
        out_specs=(whole,) * 5,
        scratch_shapes=[
            pltpu.VMEM(stored.shape, stored.dtype),
            pltpu.VMEM(adj.shape, adj.dtype),
            pltpu.SemaphoreType.DMA((3, PARTS)),
        ],
        compiler_params=FIRST_BIG,
        cost_estimate=cost(5_000_000, 4_000_000),
    )(stored, adj)
    across, along = exchange_z(across, along)
    weight, hot, acc, near = pl.pallas_call(
        stage_a,
        out_shape=(
            shape(9, slots),
            jax.ShapeDtypeStruct((Y, slots), jnp.bfloat16),
            shape(3, 8, slots),
            shape(19, len(NEAR), Z, Y),
        ),
        in_specs=[pl.BlockSpec(memory_space=pltpu.SMEM)] + [hbm] + [whole] * 3,
        scratch_shapes=[
            pltpu.VMEM(adj.shape, adj.dtype),
            pltpu.VMEM((6 * X * Z, Y), jnp.bfloat16),
            pltpu.SemaphoreType.DMA((GROUPS,)),
        ],
        compiler_params=MID,
        cost_estimate=cost(800_000_000, 2_000_000),
    )(marker_count, adj, rho, cell, marker_weight)
    to_left, to_right, across, along, low, high = pl.pallas_call(
        pack_x,
        out_shape=(shape(XROWS, Y),) * 4 + (shape(ZROWS, Y),) * 2,
        in_specs=[whole] * 6 + [any_space],
        compiler_params=PARAMS,
        cost_estimate=cost(1_000_000, 2_000_000),
    )(near, rho, to_low, to_high, along, across, acc)
    across, along = exchange_x(across, along)
    acc, which, share = pl.pallas_call(
        stage_b,
        out_shape=(
            shape(3, 8, slots),
            jax.ShapeDtypeStruct((slots, PANELS), jnp.bfloat16),
            shape(40, slots),
        ),
        scratch_shapes=[pltpu.VMEM((24 * X, Y), jnp.bfloat16)],
        compiler_params=PARAMS,
        cost_estimate=cost(400_000_000, 2_000_000),
    )(to_low, to_high, low, high, cell, panel, weight, hot, acc)
    out, token, ends_stored = pl.pallas_call(
        interior,
        out_shape=(shape(19, X, Z, Y), shape(8, PANELS), shape(2, 19, Z, Y)),
        out_specs=(hbm, whole, whole),
        scratch_shapes=[
            pltpu.VMEM(adj.shape, adj.dtype),
            pltpu.SemaphoreType.DMA((GROUPS,)),
        ],
        compiler_params=PARAMS,
        cost_estimate=cost(10_000_000, 7_000_000),
    )(stored, adj, low, high, acc)
    grad, partial, left, right = pl.pallas_call(
        stage_c,
        out_shape=(
            shape(3, slots),
            shape(lax.axis_size(FIRST), 1, 3 * PANELS),
            shape(XROWS, Y),
            shape(XROWS, Y),
        ),
        scratch_shapes=[
            pltpu.VMEM((6 * 48, Y), jnp.bfloat16),
            pltpu.VMEM((16, slots), jnp.bfloat16),
        ],
        compiler_params=PARAMS,
        cost_estimate=cost(300_000_000, 2_000_000),
    )(rho, to_left, to_right, low, high, along, across, share, hot, which, acc, token)
    partial = summed(lax.all_to_all(partial, FIRST, 0, 0), lax.axis_size(SECOND))
    partial = lax.all_to_all(partial, SECOND, 0, 0)
    return pl.pallas_call(
        finish,
        out_shape=(shape(19, X, Z, Y), shape(3, slots), shape(3, PANELS)),
        in_specs=[whole] * 8 + [any_space],
        out_specs=(any_space, hbm, hbm),
        scratch_shapes=[
            pltpu.VMEM((2, 19, Z, Y), jnp.float32),
            pltpu.VMEM((3, PANELS), jnp.float32),
            pltpu.SemaphoreType.DMA((4,)),
        ],
        input_output_aliases={8: 0},
        compiler_params=PARAMS,
        cost_estimate=cost(1_000_000, 2_000_000),
    )(partial, grad, near, ends_stored, low, high, left, right, out)


def solution(mesh):
    split = jax.sharding.Mesh(
        mesh.devices.reshape(4, 4, 4, 2, 2), ("y", "zh", "x", "zl", "core")
    )
    return jax.shard_map(
        local,
        mesh=split,
        in_specs=(
            P(None, GX, GZ, None),
            P(None, GX, GZ, None),
            P(GX + GZ),
            P(None, GX + GZ),
            P(GX + GZ),
            P(GX + GZ),
        ),
        out_specs=(P(None, GX, GZ, None), P(None, GX + GZ), P()),
        check_vma=False,
    )
```
